256 devices in a mesh: context: 32 (over z, y), tensor: 8 (over x, core).
Axes of the slice: x: 4, y: 4, z: 8, core: 2. Of those that a mesh axis runs over, the one named last changes fastest.
Arguments:
- stream: bfloat16 [8192, 8192], P('context', 'tensor'), may hold values from -12.5 to 12.5
- pre_gates: bfloat16 [3, 8192, 8192], P(None, 'context', 'tensor'), may hold values from -4 to 4
- post_gates: bfloat16 [3, 8192, 8192], P(None, 'context', 'tensor'), may hold values from -4 to 4
- norm_gains: float32 [3, 8192], P(None, 'tensor'), may hold values from 0.1 to 1.9
- se_taps: float32 [7, 8192], P(None, 'tensor'), may hold values from -2 to 2
- mr_taps: float32 [128, 8192], P(None, 'tensor'), may hold values from -0.5 to 0.5
- li_residues: float32 [8192, 16], P('tensor'), may hold values from -1.5 to 1.5
- li_decays: float32 [8192, 16], P('tensor'), may hold values from 3.0517578e-05 to 0.05
- cotangent: bfloat16 [8192, 8192], P('context', 'tensor'), may hold values from -6 to 6
Outputs:
- layer_output: bfloat16 [8192, 8192], P('context', 'tensor')
- stream_grad: bfloat16 [8192, 8192], P('context', 'tensor')
The draws below stay inside these ranges and needn't reach their ends.
All inputs are finite; a program needn't handle non-finite values.
Results may differ from the reference program's by a relative error of at most 0.017.
Values may be sent and summed in bfloat16 or wider, within the bound.
A program may use at most 128 MiB of HBM per device.

```python
import math
import jax
import jax.numpy as jnp
from jax import lax

D = 8192
SE_TAPS = 7
MR_TAPS = 128
ORDER = 16
SEQ = 8192


def draw_stream(key, part):
    key = jax.random.fold_in(key, 11)
    key_base, key_cols, key_rows = jax.random.split(key, 3)
    columns = jnp.arange(D, dtype=jnp.float32) / D
    base_values = jnp.clip(jax.random.normal(key_base, (SEQ, D), jnp.float32), -5.0, 5.0)
    rising = 0.6 * jnp.exp(0.55 * columns)
    rough_cols = jnp.exp(jax.random.uniform(key_cols, (D,), jnp.float32, -0.35, 0.35))
    row_scales = jnp.exp(jax.random.uniform(key_rows, (SEQ, 1), jnp.float32, -0.5, 0.5))
    return (base_values * rising[None, :] * rough_cols[None, :] * row_scales).astype(jnp.bfloat16)


def level_of(key, extent, pieces, low, high):
    level = 1.0
    for dim, blocks in pieces:
        heights = jax.random.uniform(jax.random.fold_in(jax.random.fold_in(key, 6), dim), (blocks,), jnp.float32, low / len(pieces), high / len(pieces))
        level = level * jnp.repeat(jnp.exp(heights), extent[dim] // blocks).reshape((-1,) + (1,) * (len(extent) - 1 - dim))
    return level


def centred(stream_key, extent, scale, bound, pieces=(), held_as=jnp.bfloat16):
    level = level_of(stream_key, extent, pieces, -0.22, 0.18) if pieces else 1.0
    drawn = jax.random.normal(stream_key, extent, jnp.float32) * scale * level
    return jnp.minimum(jnp.maximum(drawn, -bound), bound).astype(held_as)


def setup_inputs(seed: int = 0) -> dict:
    seeds = jax.random.split(jax.random.key(seed), 10)
    return {
        "stream": draw_stream(jax.random.fold_in(seeds[9], 71), 0),
        "pre_gates": centred(seeds[1], (3, SEQ, D), 1.0, 4.0, ((1, 32), (2, 8))),
        "post_gates": centred(seeds[2], (3, SEQ, D), 1.0, 4.0, ((1, 32), (2, 8))),
        "norm_gains": jnp.clip(1.0 + 0.18 * jax.random.normal(seeds[3], (3, D), jnp.float32), 0.1, 1.9),
        "se_taps": centred(seeds[4], (SE_TAPS, D), SE_TAPS ** -0.5, 2.0, ((1, 8),), jnp.float32),
        "mr_taps": centred(seeds[5], (MR_TAPS, D), MR_TAPS ** -0.5, 0.5, ((1, 8),), jnp.float32),
        "li_residues": centred(seeds[6], (D, ORDER), ORDER ** -0.5, 1.5, ((0, 8),), jnp.float32),
        "li_decays": jnp.clip(jnp.exp(math.log(0.05) - 7.4014754 * jax.random.uniform(seeds[7], (D, ORDER), jnp.float32) ** level_of(seeds[7], (D, ORDER), ((0, 8),), -0.2, 0.2)), 3.0517578125e-05, 0.05),
        "cotangent": centred(seeds[8], (SEQ, D), 1.0, 6.0, ((0, 32), (1, 8))),
    }


epsilon = 1e-06

def depthwise(padded, kernel):
    taps = kernel.shape[0]
    rows = padded.shape[0] - taps + 1

    def add_tap(index, total):
        where = index.astype(jnp.int32)
        window = lax.dynamic_slice_in_dim(padded, where, rows, 0)
        weight = lax.dynamic_slice_in_dim(kernel, where, 1, 0)
        return total + window * weight
    return lax.fori_loop(0, taps, add_tap, jnp.zeros((rows, padded.shape[1]), jnp.float32))

def causal_conv(signal, filter_taps):
    rim_rows = filter_taps.shape[0] - 1
    padded = jnp.concatenate([jnp.zeros((rim_rows, signal.shape[1]), jnp.float32), signal.astype(jnp.float32)], axis=0)
    return depthwise(padded, filter_taps[::-1])

def causal_adjoint(signal, filter_taps):
    rim_rows = filter_taps.shape[0] - 1
    padded = jnp.concatenate([signal.astype(jnp.float32), jnp.zeros((rim_rows, signal.shape[1]), jnp.float32)], axis=0)
    return depthwise(padded, filter_taps)

def filter_weights(li_residues, li_decays):
    return li_residues * jnp.sqrt(-jnp.expm1(-2.0 * li_decays))

def long_conv(signal, li_residues, li_decays, adjoint):
    block_size = 128
    block_count = D // block_size
    positions = jnp.arange(SEQ, dtype=jnp.float32)
    signals = signal.astype(jnp.float32).reshape(SEQ, block_count, block_size).transpose(1, 0, 2)
    weights_all = filter_weights(li_residues, li_decays).reshape(block_count, block_size, ORDER)
    rates_all = li_decays.reshape(block_count, block_size, ORDER)

    def convolve_block(entries):
        signal_part, weight_part, decay_rates = entries
        decay_table = jnp.exp(-decay_rates[None, :, :] * positions[:, None, None])
        kernel = lax.optimization_barrier(jnp.sum(weight_part[None] * decay_table, axis=2))
        spec_kernel = jnp.fft.rfft(kernel, n=2 * SEQ, axis=0)
        spec_signal = jnp.fft.rfft(signal_part, n=2 * SEQ, axis=0)
        if adjoint:
            product = jnp.conj(spec_kernel) * spec_signal
        else:
            product = spec_kernel * spec_signal
        return jnp.fft.irfft(product, n=2 * SEQ, axis=0)[:SEQ].astype(jnp.float32)
    result = lax.map(convolve_block, (signals, weights_all, rates_all))
    return result.transpose(1, 0, 2).reshape(SEQ, D)

def reference(stream, pre_gates, post_gates, norm_gains, se_taps, mr_taps, li_residues, li_decays, cotangent):
    kernels = (se_taps, mr_taps)
    history = []
    current = stream
    for layer in range(3):
        values = current.astype(jnp.float32)
        norm_scale = lax.rsqrt(lax.optimization_barrier(jnp.sum(values * values, axis=1, keepdims=True)) / D + epsilon)
        mixed = (pre_gates[layer].astype(jnp.float32) * values * norm_scale * norm_gains[layer]).astype(jnp.bfloat16)
        if layer < 2:
            conv_out = causal_conv(mixed, kernels[layer])
        else:
            rounded = lax.optimization_barrier(long_conv(mixed, li_residues, li_decays, False).astype(jnp.bfloat16))
            conv_out = rounded.astype(jnp.float32)
        history.append((values, norm_scale))
        current = (values + post_gates[layer].astype(jnp.float32) * conv_out).astype(jnp.bfloat16)
    gradient = cotangent
    for layer in (2, 1, 0):
        values, norm_scale = history[layer]
        gated_back = (post_gates[layer].astype(jnp.float32) * gradient.astype(jnp.float32)).astype(jnp.bfloat16)
        if layer < 2:
            spread = causal_adjoint(gated_back, kernels[layer])
        else:
            rounded = lax.optimization_barrier(long_conv(gated_back, li_residues, li_decays, True).astype(jnp.bfloat16))
            spread = rounded.astype(jnp.float32)
        upstream = spread * pre_gates[layer].astype(jnp.float32) * norm_gains[layer]
        normed = values * norm_scale
        projection = lax.optimization_barrier(jnp.sum(upstream * normed, axis=1, keepdims=True)) / D
        gradient = (gradient.astype(jnp.float32) + (upstream - normed * projection) * norm_scale).astype(jnp.bfloat16)
    return (current, gradient)
```

```python
import functools
import math

import jax
import jax.numpy as jnp
import numpy as np
from jax import lax
from jax.experimental import pallas as pl
from jax.experimental.pallas import tpu as pltpu
from jax.sharding import PartitionSpec as P

EPSILON = 1e-06
F32 = jnp.float32
BF16 = jnp.bfloat16
MESH = pl.DeviceIdType.MESH
ROWS = 256
HALF = 128
LANE = 128
WIDE = 256
POLES = 16
YN = 4


def dft_matrix(points, used):
    freqs = (2 * np.arange(points // 2)[:, None] + 1) * np.arange(used)[None, :] % (2 * points)
    angle = freqs * (math.pi / points)
    return np.concatenate([np.cos(angle), -np.sin(angle)], axis=0)


def lanes(index, width=LANE):
    return pl.ds(pl.multiple_of(index * width, width), width)


def dot(a, b):
    return jnp.dot(a, b, preferred_element_type=F32)


def split(value):
    high = value.astype(BF16)
    return high, (value - high.astype(F32)).astype(BF16)


def kernel(
    zn,
    tn,
    channels,
    stream_h, pre_h, post_h, gains_h, se_h, mr_h, res_h, dec_h, cot_h, w1_h, v1_h, w2_h, v2_h,
    out_h, grad_h,
    x0, pre, post, gains, se, mr, res, dec, cot, w1, v1, w2, v2,
    x1, x2, a0, e0, a1, e1, e2, a2, u0, u1, u2, g1, g2, local, out, grad,
    dect, weight, decb, pow8, taps, h1, h2,
    sums, sums2, col_s, col_k, psa, psb,
    st_b, st_f, r1_b, r1_f, tz_b, tz_f, r2_b, r2_f, o3_b, o3_f, r3_b, r3_f,
    load_sem, store_sem, ps_send, ps_recv, halo_send, halo_recv,
    sc1_send, sc1_recv, sc2_send, sc2_recv, sc3_send, sc3_recv,
):
    k = lax.axis_index("context")
    me = lax.axis_index("tensor")
    kn = zn * YN
    z = k // YN
    y = k % YN
    width = x0.shape[1]
    tiles = width // LANE
    chunks = width // WIDE
    following = (k + 1) % kn
    preceding = (k + kn - 1) % kn

    plan = [
        (stream_h, x0), (dec_h, dec), (res_h, res), (cot_h, cot), (post_h.at[2], post.at[2]),
        (w1_h, w1), (mr_h, mr), (gains_h, gains), (se_h, se), (w2_h, w2), (v2_h, v2), (v1_h, v1),
        (pre_h.at[0], pre.at[0]), (post_h.at[0], post.at[0]), (pre_h.at[1], pre.at[1]),
        (post_h.at[1], post.at[1]), (pre_h.at[2], pre.at[2]),
    ]
    loads = [pltpu.make_async_copy(s, d, load_sem.at[i]) for i, (s, d) in enumerate(plan)]
    for load in loads:
        load.start()

    r2_b[...] = jnp.zeros_like(r2_b)
    r2_f[...] = jnp.zeros_like(r2_f)

    barrier = pltpu.get_barrier_semaphore()
    partners = [{"tensor": (me + d) % tn} for d in range(1, tn)]
    partners += [{"context": z * YN + (y + d) % YN} for d in range(1, YN)]
    partners += [{"context": ((z + d) % zn) * YN + y} for d in range(1, zn)]
    partners += [{"context": following}, {"context": preceding}]
    for partner in partners:
        pl.semaphore_signal(barrier, inc=1, device_id=partner, device_id_type=MESH)

    def row_of(total):
        return jnp.sum(total.T, axis=0, keepdims=True)

    def col_of(row):
        return jnp.broadcast_to(row, (LANE, ROWS)).T

    def exchange(slots, phase):
        sent = []
        for d in range(1, tn):
            sent.append(
                pltpu.make_async_remote_copy(
                    src_ref=slots.at[me],
                    dst_ref=slots.at[me],
                    send_sem=ps_send.at[phase, d],
                    recv_sem=ps_recv.at[phase, d],
                    device_id={"tensor": (me + d) % tn},
                    device_id_type=MESH,
                )
            )
        return sent

    def collect(sent, slots):
        for copy in sent:
            copy.wait_send()
        for copy in sent:
            copy.wait_recv()
        total = slots[0]
        for index in range(1, tn):
            total = total + slots[index]
        return total

    def halo(src, dst, index, target):
        return pltpu.make_async_remote_copy(
            src_ref=src,
            dst_ref=dst,
            send_sem=halo_send.at[index],
            recv_sem=halo_recv.at[index],
            device_id={"context": target},
            device_id_type=MESH,
        )

    def pole_tables():
        for part in range(tiles):
            here = slice(part * LANE, (part + 1) * LANE)
            dect[:, here] = dec[here, :].T
            weight[:, here] = res[here, :].T
        rate = dect[...]
        square = rate * rate
        series = rate * (
            1.0 + square * (1.0 / 6.0) * (1.0 + square * (1.0 / 20.0) * (1.0 + square * (1.0 / 42.0)))
        )
        weight[...] = weight[...] * jnp.sqrt(2.0 * jnp.exp(-rate) * series)
        for r in range(POLES):
            wide = jnp.broadcast_to(dect[r : r + 1, :], (8, width))
            decb[r] = wide
            pow8[r] = jnp.exp(-8.0 * wide)

    def sublane():
        return lax.broadcasted_iota(jnp.int32, (1, 8, LANE), 1).astype(F32)

    def states(src, dst, reverse):
        def quarter(q, carry):
            for side in range(2):
                where = lanes(q * 2 + side)
                base = pow8[:, :, where]
                total = jnp.zeros((POLES, 8, LANE), F32)

                def step(g, total):
                    group = (ROWS // 16 - 1 - g) if reverse else g
                    rows = pl.ds(pl.multiple_of(group * 16, 16), 16)
                    value = src[rows, where].astype(F32)
                    first, second = (value[8:], value[:8]) if reverse else (value[:8], value[8:])
                    total = total * base + first[None]
                    return total * base + second[None]

                total = lax.fori_loop(0, ROWS // 16, step, total)
                place = sublane() if reverse else 7.0 - sublane()
                total = total * jnp.exp(-decb[:, :, where] * place)
                dst[q, :, side * LANE : (side + 1) * LANE] = jnp.sum(total, axis=1)
            return carry

        lax.fori_loop(0, chunks, quarter, 0)

    def spread_poles(start, base, reverse, sink):
        def step(g, state):
            group = (ROWS // 16 - 1 - g) if reverse else g
            rows = pl.ds(pl.multiple_of(group * 16, 16), 16)
            first = jnp.sum(state, axis=0)
            state = state * base
            second = jnp.sum(state, axis=0)
            state = state * base
            pair = [second, first] if reverse else [first, second]
            sink(rows, jnp.concatenate(pair, axis=0))
            return state

        lax.fori_loop(0, ROWS // 16, step, start)

    def stacked(ref, index, where):
        return jnp.stack(
            [jnp.broadcast_to(ref[index, r : r + 1, where], (8, LANE)) for r in range(POLES)]
        )

    def stacked_flat(ref, where):
        return jnp.stack(
            [jnp.broadcast_to(ref[r : r + 1, where], (8, LANE)) for r in range(POLES)]
        )

    def filter_head():
        def tile(t, carry):
            where = lanes(t)
            start = stacked_flat(weight, where) * jnp.exp(-decb[:, :, where] * sublane())

            def sink(rows, value):
                taps[rows, where] = value

            spread_poles(start, pow8[:, :, where], False, sink)
            return carry

        lax.fori_loop(0, tiles, tile, 0)

    def spectra(matrix, source, dst, used):
        def chunk(q, carry):
            where = lanes(q, WIDE)
            high, low = split(source[:, where])
            table = matrix[:, :used]
            dst[:, where] = dot(table, high) + dot(table, low)
            return carry

        lax.fori_loop(0, chunks, chunk, 0)

    def filtered(matrix, back, window, spectrum, adjoint):
        half = matrix.shape[0] // 2
        image = dot(matrix[...], window)
        re, im = image[:half], image[half:]
        hre, him = spectrum[:half], spectrum[half:]
        if adjoint:
            out_re = re * hre + im * him
            out_im = im * hre - re * him
        else:
            out_re = re * hre - im * him
            out_im = re * him + im * hre
        product = jnp.concatenate([out_re.astype(BF16), out_im.astype(BF16)], axis=0)
        return dot(back, product)

    def local_part(src, adjoint):
        def chunk(q, carry):
            where = lanes(q, WIDE)
            local[:, where] = filtered(w2, v2[...], src[:, where], h2[:, where], adjoint)
            return carry

        lax.fori_loop(0, chunks, chunk, 0)

    def scan_one(st, r1, line):
        sent = []
        for d in range(1, YN):
            other = (y + d) % YN
            sent.append(
                pltpu.make_async_remote_copy(
                    src_ref=st.at[other],
                    dst_ref=r1.at[y],
                    send_sem=sc1_send.at[line, d],
                    recv_sem=sc1_recv.at[line, d],
                    device_id={"context": z * YN + other},
                    device_id_type=MESH,
                )
            )
        for copy in sent:
            copy.start()
        r1[y] = st[y]
        return sent

    def finish(sent):
        for copy in sent:
            copy.wait_send()
        for copy in sent:
            copy.wait_recv()

    def rate_here():
        return dect[:, lanes(y, WIDE)]

    def scan_two(sent, r1, tz, r2, line, reverse):
        finish(sent)
        step = jnp.exp(-float(ROWS) * rate_here())
        order = range(YN - 1, -1, -1) if reverse else range(YN)
        total = jnp.zeros((POLES, WIDE), F32)
        for index in order:
            total = total * step + r1[index]
        tz[...] = total
        moved = []
        for d in range(1, zn):
            target = z - d if reverse else z + d
            source = z + d if reverse else z - d
            copy = pltpu.make_async_remote_copy(
                src_ref=tz,
                dst_ref=r2.at[z],
                send_sem=sc2_send.at[line, d],
                recv_sem=sc2_recv.at[line, d],
                device_id={"context": ((target + zn) % zn) * YN + y},
                device_id_type=MESH,
            )
            sends = (target >= 0) if reverse else (target < zn)
            gets = (source < zn) if reverse else (source >= 0)

            @pl.when(sends)
            def _(copy=copy):
                copy.start()

            moved.append((copy, sends, gets))
        return moved

    def scan_three(moved, r1, r2, o3, r3, line, reverse):
        for copy, sends, gets in moved:

            @pl.when(sends)
            def _(copy=copy):
                copy.wait_send()

            @pl.when(gets)
            def _(copy=copy):
                copy.wait_recv()

        rate = rate_here()
        step = jnp.exp(-float(ROWS) * rate)
        group = jnp.exp(-float(ROWS * YN) * rate)
        state = jnp.zeros((POLES, WIDE), F32)
        for d in range(zn - 1, 0, -1):
            source = (z + d) if reverse else (z - d)
            state = state * group + r2[(source + zn) % zn]
        order = range(YN - 1, -1, -1) if reverse else range(YN)
        for index in order:
            o3[index] = state
            state = state * step + r1[index]
        sent = []
        for d in range(1, YN):
            other = (y + d) % YN
            sent.append(
                pltpu.make_async_remote_copy(
                    src_ref=o3.at[other],
                    dst_ref=r3.at[y],
                    send_sem=sc3_send.at[line, d],
                    recv_sem=sc3_recv.at[line, d],
                    device_id={"context": z * YN + other},
                    device_id_type=MESH,
                )
            )
        for copy in sent:
            copy.start()
        r3[y] = o3[y]
        return sent

    def carried(r3, reverse, sink):
        def quarter(q, carry):
            for side in range(2):
                where = lanes(q * 2 + side)
                inner = slice(side * LANE, (side + 1) * LANE)
                place = (8.0 - sublane()) if reverse else (sublane() + 1.0)
                start = (
                    stacked(r3, q, inner)
                    * stacked_flat(weight, where)
                    * jnp.exp(-decb[:, :, where] * place)
                )
                spread_poles(
                    start, pow8[:, :, where], reverse, lambda rows, value: sink(rows, where, value)
                )
            return carry

        lax.fori_loop(0, chunks, quarter, 0)

    def over_tiles(body):
        def step(t, carry):
            body(lanes(t), t)
            return carry

        lax.fori_loop(0, tiles, step, 0)

    def over_chunks(body):
        def step(q, carry):
            body(lanes(q, WIDE))
            return carry

        lax.fori_loop(0, chunks, step, 0)

    def fold(value):
        return sum(value[:, i * LANE : (i + 1) * LANE] for i in range(value.shape[1] // LANE))

    def twice(column):
        return jnp.concatenate([column] * (WIDE // LANE), axis=1)

    loads[0].wait()
    sums[...] = jnp.zeros_like(sums)

    def square_stream(where, t):
        value = x0[:, where].astype(F32)
        sums[...] += value * value

    over_tiles(square_stream)
    psa[0, me] = row_of(sums[...])

    for load in loads[1:5]:
        load.wait()
    pole_tables()

    def cotangent_gate(where, t):
        e2[:, where] = (post[2, :, where].astype(F32) * cot[:, where].astype(F32)).astype(BF16)

    over_tiles(cotangent_gate)
    states(e2, st_b, True)

    pl.semaphore_wait(barrier, len(partners))
    first_sum = exchange(psa.at[0], 0)
    for copy in first_sum:
        copy.start()
    back_one = scan_one(st_b, r1_b, 0)
    for load in loads[5:]:
        load.wait()
    spectra(w1, mr, h1, HALF)

    total = collect(first_sum, psa.at[0])
    s0 = lax.rsqrt(total * (1.0 / channels) + EPSILON)
    col_s[0] = col_of(s0)

    def gate_stream(where, t, rows):
        value = (
            pre[0, rows, where].astype(F32)
            * x0[rows, where].astype(F32)
            * col_s[0, rows, :]
            * gains[0:1, where]
        )
        a0[t, pl.ds(rows.start + 8, rows.stop - rows.start), :] = value.astype(BF16).astype(F32)

    over_tiles(lambda where, t: gate_stream(where, t, slice(240, 256)))
    short_halo = halo(a0.at[:, pl.ds(256, 8), :], a0.at[:, pl.ds(0, 8), :], 0, following)
    short_halo.start()
    over_tiles(lambda where, t: gate_stream(where, t, slice(0, 240)))

    def short_layer(where, t, first, count):
        conv = se[0:1, where] * a0[t, pl.ds(first + 8, count), :]
        for j in range(1, 7):
            conv += se[j : j + 1, where] * a0[t, pl.ds(first + 8 - j, count), :]
        rows = slice(first, first + count)
        value = (x0[rows, where].astype(F32) + post[0, rows, where].astype(F32) * conv).astype(BF16)
        x1[rows, where] = value
        value = value.astype(F32)
        sums[rows, :] += value * value

    sums[...] = jnp.zeros_like(sums)
    over_tiles(lambda where, t: short_layer(where, t, 16, 240))
    short_halo.wait()

    @pl.when(k == 0)
    def _():
        a0[:, 0:8, :] = jnp.zeros((tiles, 8, LANE), F32)

    over_tiles(lambda where, t: short_layer(where, t, 0, 16))
    psa[1, me] = row_of(sums[...])
    second_sum = exchange(psa.at[1], 1)
    for copy in second_sum:
        copy.start()

    back_two = scan_two(back_one, r1_b, tz_b, r2_b, 0, True)
    filter_head()
    spectra(w2, taps, h2, ROWS)

    total = collect(second_sum, psa.at[1])
    s1 = lax.rsqrt(total * (1.0 / channels) + EPSILON)
    col_s[1] = col_of(s1)

    def gate_medium(where, t, rows):
        value = (
            pre[1, rows, where].astype(F32)
            * x1[rows, where].astype(F32)
            * col_s[1, rows, :]
            * gains[1:2, where]
        )
        a1[pl.ds(rows.start + HALF, HALF), where] = value.astype(BF16)

    over_tiles(lambda where, t: gate_medium(where, t, slice(HALF, ROWS)))
    medium_halo = halo(a1.at[pl.ds(ROWS, HALF), :], a1.at[pl.ds(0, HALF), :], 1, following)
    medium_halo.start()
    over_tiles(lambda where, t: gate_medium(where, t, slice(0, HALF)))
    back_three = scan_three(back_two, r1_b, r2_b, o3_b, r3_b, 0, True)

    def medium_layer(where, rows):
        window = a1[pl.ds(rows.start, ROWS), where]
        conv = filtered(w1, v1[HALF:, :], window, h1[:, where], False)
        value = x1[rows, where].astype(F32) + post[1, rows, where].astype(F32) * conv
        x2[rows, where] = value.astype(BF16)

    over_chunks(lambda where: medium_layer(where, slice(HALF, ROWS)))
    local_part(e2, True)
    finish(back_three)

    def back_long(rows, where, value):
        spread = (local[rows, where] + value).astype(BF16).astype(F32)
        u2[rows, where] = spread * pre[2, rows, where].astype(F32) * gains[2:3, where]

    carried(r3_b, True, back_long)
    medium_halo.wait()

    @pl.when(k == 0)
    def _():
        a1[0:HALF, :] = jnp.zeros((HALF, width), BF16)

    over_chunks(lambda where: medium_layer(where, slice(0, HALF)))
    sums[...] = jnp.zeros_like(sums)
    sums2[...] = jnp.zeros_like(sums2)

    def both_sums(where, t):
        value = x2[:, where].astype(F32)
        sums[...] += value * value
        sums2[...] += value * u2[:, where]

    over_tiles(both_sums)
    psb[me] = jnp.concatenate([row_of(sums[...]), row_of(sums2[...])], axis=0)
    third_sum = exchange(psb, 2)
    for copy in third_sum:
        copy.start()
    total = collect(third_sum, psb)
    s2 = lax.rsqrt(total[0:1] * (1.0 / channels) + EPSILON)
    col_s[2] = col_of(s2)
    col_k[...] = col_of(s2 * s2 * s2 * total[1:2] * (1.0 / channels))

    def back_two_rows(where, t, rows):
        value = (
            cot[rows, where].astype(F32)
            + u2[rows, where] * col_s[2, rows, :]
            - x2[rows, where].astype(F32) * col_k[rows, :]
        ).astype(BF16)
        g2[rows, where] = value
        e1[rows, where] = (post[1, rows, where].astype(F32) * value.astype(F32)).astype(BF16)

    over_tiles(lambda where, t: back_two_rows(where, t, slice(0, HALF)))
    medium_back = halo(e1.at[pl.ds(0, HALF), :], e1.at[pl.ds(ROWS, HALF), :], 2, preceding)
    medium_back.start()
    over_tiles(lambda where, t: back_two_rows(where, t, slice(HALF, ROWS)))

    def gate_long(where, t):
        value = (
            pre[2, :, where].astype(F32)
            * x2[:, where].astype(F32)
            * col_s[2]
            * gains[2:3, where]
        )
        a2[:, where] = value.astype(BF16)

    over_tiles(gate_long)
    states(a2, st_f, False)
    fore_one = scan_one(st_f, r1_f, 1)

    sums[...] = jnp.zeros_like(sums)

    def medium_adjoint(where, rows):
        window = e1[pl.ds(rows.start, ROWS), where]
        spread = filtered(w1, v1[:HALF, :], window, h1[:, where], True)
        value = spread * pre[1, rows, where].astype(F32) * gains[1:2, where]
        u1[rows, where] = value
        sums[rows, :] += fold(value * x1[rows, where].astype(F32))

    over_chunks(lambda where: medium_adjoint(where, slice(0, HALF)))
    fore_two = scan_two(fore_one, r1_f, tz_f, r2_f, 1, False)
    medium_back.wait()

    @pl.when(k == kn - 1)
    def _():
        e1[ROWS : ROWS + HALF, :] = jnp.zeros((HALF, width), BF16)

    over_chunks(lambda where: medium_adjoint(where, slice(HALF, ROWS)))
    psa[2, me] = row_of(sums[...])
    fourth_sum = exchange(psa.at[2], 3)
    for copy in fourth_sum:
        copy.start()
    local_part(a2, False)
    total = collect(fourth_sum, psa.at[2])
    col_k[...] = col_of(s1 * s1 * s1 * total * (1.0 / channels))

    def back_one_rows(where, t, rows):
        value = (
            g2[rows, where].astype(F32)
            + u1[rows, where] * col_s[1, rows, :]
            - x1[rows, where].astype(F32) * col_k[rows, :]
        ).astype(BF16)
        g1[rows, where] = value
        e0[t, rows, :] = (
            (post[0, rows, where].astype(F32) * value.astype(F32)).astype(BF16).astype(F32)
        )

    over_tiles(lambda where, t: back_one_rows(where, t, slice(0, 16)))
    short_back = halo(e0.at[:, pl.ds(0, 8), :], e0.at[:, pl.ds(256, 8), :], 3, preceding)
    short_back.start()
    over_tiles(lambda where, t: back_one_rows(where, t, slice(16, ROWS)))
    sums[...] = jnp.zeros_like(sums)

    def short_adjoint(where, t, first, count):
        spread = se[0:1, where] * e0[t, pl.ds(first, count), :]
        for j in range(1, 7):
            spread += se[j : j + 1, where] * e0[t, pl.ds(first + j, count), :]
        rows = slice(first, first + count)
        value = spread * pre[0, rows, where].astype(F32) * gains[0:1, where]
        u0[rows, where] = value
        sums[rows, :] += value * x0[rows, where].astype(F32)

    over_tiles(lambda where, t: short_adjoint(where, t, 0, 240))
    short_back.wait()

    @pl.when(k == kn - 1)
    def _():
        e0[:, 256:264, :] = jnp.zeros((tiles, 8, LANE), F32)

    over_tiles(lambda where, t: short_adjoint(where, t, 240, 16))
    psa[3, me] = row_of(sums[...])
    fifth_sum = exchange(psa.at[3], 4)
    for copy in fifth_sum:
        copy.start()

    fore_three = scan_three(fore_two, r1_f, r2_f, o3_f, r3_f, 1, False)
    total = collect(fifth_sum, psa.at[3])
    col_k[...] = col_of(s0 * s0 * s0 * total * (1.0 / channels))

    def final_rows(where, t):
        value = (
            g1[:, where].astype(F32)
            + u0[:, where] * col_s[0]
            - x0[:, where].astype(F32) * col_k[...]
        )
        grad[:, where] = value.astype(BF16)

    over_tiles(final_rows)
    store_grad = pltpu.make_async_copy(grad, grad_h, store_sem.at[0])
    store_grad.start()
    finish(fore_three)

    def fore_long(rows, where, value):
        conv = (local[rows, where] + value).astype(BF16).astype(F32)
        result = x2[rows, where].astype(F32) + post[2, rows, where].astype(F32) * conv
        out[rows, where] = result.astype(BF16)

    carried(r3_f, False, fore_long)
    store_out = pltpu.make_async_copy(out, out_h, store_sem.at[1])
    store_out.start()
    store_grad.wait()
    store_out.wait()


def per_device(zn, tn, *args):
    stream, pre, post, gains, se, mr, res, dec, cot = args
    width = stream.shape[1]
    channels = width * tn
    tiles = width // LANE
    tables = (
        jnp.asarray(dft_matrix(WIDE, WIDE), BF16),
        jnp.asarray(dft_matrix(WIDE, WIDE).T * (2.0 / WIDE), BF16),
        jnp.asarray(dft_matrix(2 * ROWS, ROWS), BF16),
        jnp.asarray(dft_matrix(2 * ROWS, ROWS).T * (1.0 / ROWS), BF16),
    )
    operands = (stream, pre, post, gains, se, mr, res, dec, cot) + tables
    vmem = pltpu.VMEM
    whole = (ROWS, width)
    scan = (YN, POLES, WIDE)
    scratch = [vmem(o.shape, o.dtype) for o in operands]
    scratch += [
        vmem(whole, BF16),
        vmem(whole, BF16),
        vmem((tiles, ROWS + 8, LANE), F32),
        vmem((tiles, ROWS + 8, LANE), F32),
        vmem((ROWS + HALF, width), BF16),
        vmem((ROWS + HALF, width), BF16),
        vmem(whole, BF16),
        vmem(whole, BF16),
        vmem(whole, F32),
        vmem(whole, F32),
        vmem(whole, F32),
        vmem(whole, BF16),
        vmem(whole, BF16),
        vmem(whole, F32),
        vmem(whole, BF16),
        vmem(whole, BF16),
        vmem((POLES, width), F32),
        vmem((POLES, width), F32),
        vmem((POLES, 8, width), F32),
        vmem((POLES, 8, width), F32),
        vmem(whole, F32),
        vmem((WIDE, width), F32),
        vmem((2 * ROWS, width), F32),
        vmem((ROWS, LANE), F32),
        vmem((ROWS, LANE), F32),
        vmem((3, ROWS, LANE), F32),
        vmem((ROWS, LANE), F32),
        vmem((4, tn, 1, ROWS), F32),
        vmem((tn, 2, ROWS), F32),
        vmem(scan, F32), vmem(scan, F32),
        vmem(scan, F32), vmem(scan, F32),
        vmem(scan[1:], F32), vmem(scan[1:], F32),
        vmem((zn, POLES, WIDE), F32), vmem((zn, POLES, WIDE), F32),
        vmem(scan, F32), vmem(scan, F32),
        vmem(scan, F32), vmem(scan, F32),
    ]
    sem = pltpu.SemaphoreType.DMA
    scratch += [
        sem((17,)), sem((2,)), sem((5, tn)), sem((5, tn)), sem((4,)), sem((4,)),
        sem((2, YN)), sem((2, YN)), sem((2, zn)), sem((2, zn)), sem((2, YN)), sem((2, YN)),
    ]
    any_spec = pl.BlockSpec(memory_space=pl.ANY)
    return pl.pallas_call(
        functools.partial(kernel, zn, tn, channels),
        out_shape=(jax.ShapeDtypeStruct(whole, BF16), jax.ShapeDtypeStruct(whole, BF16)),
        in_specs=[any_spec] * len(operands),
        out_specs=(any_spec, any_spec),
        scratch_shapes=scratch,
        compiler_params=pltpu.CompilerParams(
            collective_id=0, has_side_effects=True, vmem_limit_bytes=40 * 2**20
        ),
        cost_estimate=pl.CostEstimate(
            flops=4_000_000_000, bytes_accessed=7_000_000, transcendentals=500_000
        ),
        name="hyena_group",
    )(*operands)


def solution(mesh):
    zn = mesh.shape["context"] // YN
    tn = mesh.shape["tensor"]
    placed = (
        P("context", "tensor"),
        P(None, "context", "tensor"),
        P(None, "context", "tensor"),
        P(None, "tensor"),
        P(None, "tensor"),
        P(None, "tensor"),
        P("tensor", None),
        P("tensor", None),
        P("context", "tensor"),
    )
    return jax.shard_map(
        functools.partial(per_device, zn, tn),
        mesh=mesh,
        in_specs=placed,
        out_specs=(P("context", "tensor"), P("context", "tensor")),
        check_vma=False,
    )
```

```python
import functools
import math

import jax
import jax.numpy as jnp
import numpy as np
from jax import lax
from jax.experimental import pallas as pl
from jax.experimental.pallas import tpu as pltpu
from jax.sharding import PartitionSpec as P

EPSILON = 1e-06
F32 = jnp.float32
BF16 = jnp.bfloat16
MESH = pl.DeviceIdType.MESH
ROWS = 256
HALF = 128
LANE = 128
WIDE = 256
POLES = 16
YN = 4


def dft_matrix(points, used):
    freqs = (2 * np.arange(points // 2)[:, None] + 1) * np.arange(used)[None, :] % (2 * points)
    angle = freqs * (math.pi / points)
    return np.concatenate([np.cos(angle), -np.sin(angle)], axis=0)


def lanes(index, width=LANE):
    return pl.ds(pl.multiple_of(index * width, width), width)


def dot(a, b):
    return jnp.dot(a, b, preferred_element_type=F32)


def split(value):
    high = value.astype(BF16)
    return high, (value - high.astype(F32)).astype(BF16)


def kernel(
    zn,
    tn,
    channels,
    stream_h, pre_h, post_h, gains_h, se_h, mr_h, res_h, dec_h, cot_h, w1_h, v1_h, w2_h, v2_h,
    out_h, grad_h,
    x0, pre, post, gains, se, mr, res, dect, cot, w1, v1, w2, v2,
    x1, x2, a0, e0, a1, e1, e2, a2, u0, u1, u2, g1, g2, local, out, grad,
    weight, decb, pow8, taps, h1, h2,
    sums, sums2, col_s, col_k, ps0, psh, ps2,
    st_b, st_f, r1_b, r1_f, tz_b, tz_f, r2_b, r2_f, o3_b, o3_f, r3_b, r3_f,
    load_sem, store_sem, ps_send, ps_recv, halo_send, halo_recv,
    sc1_send, sc1_recv, sc2_send, sc2_recv, sc3_send, sc3_recv,
):
    k = lax.axis_index("context")
    me = lax.axis_index("tensor")
    kn = zn * YN
    z = k // YN
    y = k % YN
    width = x0.shape[1]
    tiles = width // LANE
    chunks = width // WIDE
    following = (k + 1) % kn
    preceding = (k + kn - 1) % kn

    plan = [
        (stream_h, x0), (dec_h, dect), (res_h, res), (cot_h, cot), (post_h.at[2], post.at[2]),
        (w1_h, w1), (mr_h, mr), (gains_h, gains), (se_h, se), (w2_h, w2), (v2_h, v2), (v1_h, v1),
        (pre_h.at[0], pre.at[0]), (post_h.at[0], post.at[0]), (pre_h.at[1], pre.at[1]),
        (post_h.at[1], post.at[1]), (pre_h.at[2], pre.at[2]),
    ]
    loads = [pltpu.make_async_copy(s, d, load_sem.at[i]) for i, (s, d) in enumerate(plan)]
    for load in loads:
        load.start()

    r2_b[...] = jnp.zeros_like(r2_b)
    r2_f[...] = jnp.zeros_like(r2_f)

    barrier = pltpu.get_barrier_semaphore()
    partners = [{"tensor": (me + d) % tn} for d in range(1, tn)]
    partners += [{"context": z * YN + (y + d) % YN} for d in range(1, YN)]
    partners += [{"context": ((z + d) % zn) * YN + y} for d in range(1, zn)]
    partners += [{"context": following}, {"context": preceding}]
    for partner in partners:
        pl.semaphore_signal(barrier, inc=1, device_id=partner, device_id_type=MESH)

    def row_of(total):
        return jnp.sum(total.T, axis=0, keepdims=True)

    def col_of(row):
        return jnp.broadcast_to(row, (LANE, row.shape[1])).T

    leaving = []

    def exchange(slots, phase):
        sent = []
        for d in range(1, tn):
            sent.append(
                pltpu.make_async_remote_copy(
                    src_ref=slots.at[me],
                    dst_ref=slots.at[me],
                    send_sem=ps_send.at[phase, d],
                    recv_sem=ps_recv.at[phase, d],
                    device_id={"tensor": (me + d) % tn},
                    device_id_type=MESH,
                )
            )
        for copy in sent:
            copy.start()
        leaving.extend(sent)
        return sent

    def collect(sent, slots):
        for copy in sent:
            copy.wait_recv()
        total = slots[0]
        for index in range(1, tn):
            total = total + slots[index]
        return total

    def halo(src, dst, index, target):
        copy = pltpu.make_async_remote_copy(
            src_ref=src,
            dst_ref=dst,
            send_sem=halo_send.at[index],
            recv_sem=halo_recv.at[index],
            device_id={"context": target},
            device_id_type=MESH,
        )
        copy.start()
        leaving.append(copy)
        return copy

    def pole_tables():
        rate = dect[...]
        square = rate * rate
        series = rate * (
            1.0 + square * (1.0 / 6.0) * (1.0 + square * (1.0 / 20.0) * (1.0 + square * (1.0 / 42.0)))
        )
        weight[...] = res[...] * jnp.sqrt(2.0 * jnp.exp(-rate) * series)
        for r in range(POLES):
            wide = jnp.broadcast_to(dect[r : r + 1, :], (8, width))
            decb[r] = wide
            pow8[r] = jnp.exp(-8.0 * wide)

    def sublane():
        return lax.broadcasted_iota(jnp.int32, (1, 8, LANE), 1).astype(F32)

    def states(src, dst, reverse):
        def quarter(q, carry):
            for side in range(2):
                where = lanes(q * 2 + side)
                base = pow8[:, :, where]
                total = jnp.zeros((POLES, 8, LANE), F32)

                def step(g, total):
                    group = (ROWS // 16 - 1 - g) if reverse else g
                    rows = pl.ds(pl.multiple_of(group * 16, 16), 16)
                    value = src[rows, where].astype(F32)
                    first, second = (value[8:], value[:8]) if reverse else (value[:8], value[8:])
                    total = total * base + first[None]
                    return total * base + second[None]

                total = lax.fori_loop(0, ROWS // 16, step, total, unroll=True)
                place = sublane() if reverse else 7.0 - sublane()
                total = total * jnp.exp(-decb[:, :, where] * place)
                dst[q, :, side * LANE : (side + 1) * LANE] = jnp.sum(total, axis=1)
            return carry

        lax.fori_loop(0, chunks, quarter, 0)

    def spread_poles(start, base, reverse, sink):
        def step(g, state):
            group = (ROWS // 16 - 1 - g) if reverse else g
            rows = pl.ds(pl.multiple_of(group * 16, 16), 16)
            first = jnp.sum(state, axis=0)
            state = state * base
            second = jnp.sum(state, axis=0)
            state = state * base
            pair = [second, first] if reverse else [first, second]
            sink(rows, jnp.concatenate(pair, axis=0))
            return state

        lax.fori_loop(0, ROWS // 16, step, start, unroll=True)

    def stacked(ref, index, where):
        return jnp.stack(
            [jnp.broadcast_to(ref[index, r : r + 1, where], (8, LANE)) for r in range(POLES)]
        )

    def stacked_flat(ref, where):
        return jnp.stack(
            [jnp.broadcast_to(ref[r : r + 1, where], (8, LANE)) for r in range(POLES)]
        )

    def filter_head():
        def tile(t, carry):
            where = lanes(t)
            start = stacked_flat(weight, where) * jnp.exp(-decb[:, :, where] * sublane())

            def sink(rows, value):
                taps[rows, where] = value

            spread_poles(start, pow8[:, :, where], False, sink)
            return carry

        lax.fori_loop(0, tiles, tile, 0)

    def spectra(matrix, source, dst, used):
        def chunk(q, carry):
            where = lanes(q, WIDE)
            high, low = split(source[:, where])
            table = matrix[:, :used]
            dst[:, where] = dot(
                jnp.concatenate([table, table], axis=1), jnp.concatenate([high, low], axis=0)
            )
            return carry

        lax.fori_loop(0, chunks, chunk, 0, unroll=True)

    def filtered(matrix, back, window, spectrum, adjoint):
        half = matrix.shape[0] // 2
        image = dot(matrix[...], window)
        re, im = image[:half], image[half:]
        hre, him = spectrum[:half], spectrum[half:]
        if adjoint:
            out_re = re * hre + im * him
            out_im = im * hre - re * him
        else:
            out_re = re * hre - im * him
            out_im = re * him + im * hre
        product = jnp.concatenate([out_re.astype(BF16), out_im.astype(BF16)], axis=0)
        return dot(back, product)

    def local_part(src, adjoint):
        def chunk(q, carry):
            where = lanes(q, WIDE)
            local[:, where] = filtered(w2, v2[...], src[:, where], h2[:, where], adjoint)
            return carry

        lax.fori_loop(0, chunks, chunk, 0, unroll=True)

    def scan_one(st, r1, line):
        sent = []
        for d in range(1, YN):
            other = (y + d) % YN
            sent.append(
                pltpu.make_async_remote_copy(
                    src_ref=st.at[other],
                    dst_ref=r1.at[y],
                    send_sem=sc1_send.at[line, d],
                    recv_sem=sc1_recv.at[line, d],
                    device_id={"context": z * YN + other},
                    device_id_type=MESH,
                )
            )
        for copy in sent:
            copy.start()
        leaving.extend(sent)
        r1[y] = st[y]
        return sent

    def finish(sent):
        for copy in sent:
            copy.wait_recv()

    def rate_here():
        return dect[:, lanes(y, WIDE)]

    def scan_two(sent, r1, tz, r2, line, reverse):
        finish(sent)
        step = jnp.exp(-float(ROWS) * rate_here())
        order = range(YN - 1, -1, -1) if reverse else range(YN)
        total = jnp.zeros((POLES, WIDE), F32)
        for index in order:
            total = total * step + r1[index]
        tz[...] = total
        moved = []
        for d in range(1, zn):
            target = z - d if reverse else z + d
            source = z + d if reverse else z - d
            copy = pltpu.make_async_remote_copy(
                src_ref=tz,
                dst_ref=r2.at[z],
                send_sem=sc2_send.at[line, d],
                recv_sem=sc2_recv.at[line, d],
                device_id={"context": ((target + zn) % zn) * YN + y},
                device_id_type=MESH,
            )
            sends = (target >= 0) if reverse else (target < zn)
            gets = (source < zn) if reverse else (source >= 0)

            @pl.when(sends)
            def _(copy=copy):
                copy.start()

            moved.append((copy, sends, gets))
        return moved

    def scan_three(moved, r1, r2, o3, r3, line, reverse):
        for copy, sends, gets in moved:

            @pl.when(gets)
            def _(copy=copy):
                copy.wait_recv()

        rate = rate_here()
        step = jnp.exp(-float(ROWS) * rate)
        group = jnp.exp(-float(ROWS * YN) * rate)
        state = jnp.zeros((POLES, WIDE), F32)
        for d in range(zn - 1, 0, -1):
            source = (z + d) if reverse else (z - d)
            state = state * group + r2[(source + zn) % zn]
        order = range(YN - 1, -1, -1) if reverse else range(YN)
        for index in order:
            o3[index] = state
            state = state * step + r1[index]
        sent = []
        for d in range(1, YN):
            other = (y + d) % YN
            sent.append(
                pltpu.make_async_remote_copy(
                    src_ref=o3.at[other],
                    dst_ref=r3.at[y],
                    send_sem=sc3_send.at[line, d],
                    recv_sem=sc3_recv.at[line, d],
                    device_id={"context": z * YN + other},
                    device_id_type=MESH,
                )
            )
        for copy in sent:
            copy.start()
        leaving.extend(sent)
        r3[y] = o3[y]
        return sent

    def carried(r3, reverse, sink):
        def quarter(q, carry):
            for side in range(2):
                where = lanes(q * 2 + side)
                inner = slice(side * LANE, (side + 1) * LANE)
                place = (8.0 - sublane()) if reverse else (sublane() + 1.0)
                start = (
                    stacked(r3, q, inner)
                    * stacked_flat(weight, where)
                    * jnp.exp(-decb[:, :, where] * place)
                )
                spread_poles(
                    start, pow8[:, :, where], reverse, lambda rows, value: sink(rows, where, value)
                )
            return carry

        lax.fori_loop(0, chunks, quarter, 0)

    def over_tiles(body):
        def step(t, carry):
            body(lanes(t), t)
            return carry

        lax.fori_loop(0, tiles, step, 0)

    def over_chunks(body):
        def step(q, carry):
            body(lanes(q, WIDE))
            return carry

        lax.fori_loop(0, chunks, step, 0, unroll=True)

    def fold(value):
        return sum(value[:, i * LANE : (i + 1) * LANE] for i in range(value.shape[1] // LANE))

    def twice(column):
        return jnp.concatenate([column] * (WIDE // LANE), axis=1)

    low = slice(0, HALF)
    high = slice(HALF, ROWS)

    def inverse(total):
        return lax.rsqrt(total * (1.0 / channels) + EPSILON)

    def clear(rows):
        sums[rows, :] = jnp.zeros((HALF, LANE), F32)
        sums2[rows, :] = jnp.zeros((HALF, LANE), F32)

    def part(q):
        return slice(q * WIDE, (q + 1) * WIDE)

    loads[0].wait()
    clear(low)
    clear(high)

    def square_stream(where, t):
        value = x0[:, where].astype(F32)
        sums[...] += value * value

    over_tiles(square_stream)
    ps0[0, me] = row_of(sums[...])

    pl.semaphore_wait(barrier, len(partners))
    sent_s0 = exchange(ps0.at[0], 0)

    for load in loads[1:5]:
        load.wait()
    pole_tables()

    def cotangent_gate(where, t):
        e2[:, where] = (post[2, :, where].astype(F32) * cot[:, where].astype(F32)).astype(BF16)

    over_tiles(cotangent_gate)
    states(e2, st_b, True)
    back_one = scan_one(st_b, r1_b, 0)
    for load in loads[5:]:
        load.wait()
    spectra(w1, mr, h1, HALF)

    s0 = inverse(collect(sent_s0, ps0.at[0]))
    col_s[0] = col_of(s0)

    def gate_stream(where, t, first, count):
        rows = slice(first, first + count)
        value = (
            pre[0, rows, where].astype(F32)
            * x0[rows, where].astype(F32)
            * col_s[0, rows, :]
            * gains[0:1, where]
        )
        a0[t, pl.ds(first + 8, count), :] = value.astype(BF16).astype(F32)

    def short_layer(where, t, first, count):
        conv = se[0:1, where] * a0[t, pl.ds(first + 8, count), :]
        for j in range(1, 7):
            conv += se[j : j + 1, where] * a0[t, pl.ds(first + 8 - j, count), :]
        rows = slice(first, first + count)
        value = (x0[rows, where].astype(F32) + post[0, rows, where].astype(F32) * conv).astype(BF16)
        x1[rows, where] = value
        value = value.astype(F32)
        sums[rows, :] += value * value

    over_tiles(lambda where, t: gate_stream(where, t, 240, 16))
    short_halo = halo(a0.at[:, pl.ds(256, 8), :], a0.at[:, pl.ds(0, 8), :], 0, following)
    over_tiles(lambda where, t: gate_stream(where, t, 112, 128))
    clear(low)
    clear(high)
    over_tiles(lambda where, t: short_layer(where, t, 128, 128))
    psh[0, me] = row_of(sums[high, :])
    sent_s1_high = exchange(psh.at[0], 1)

    back_two = scan_two(back_one, r1_b, tz_b, r2_b, 0, True)
    over_tiles(lambda where, t: gate_stream(where, t, 0, 112))
    over_tiles(lambda where, t: short_layer(where, t, 16, 112))
    filter_head()
    short_halo.wait_recv()

    @pl.when(k == 0)
    def _():
        a0[:, 0:8, :] = jnp.zeros((tiles, 8, LANE), F32)

    over_tiles(lambda where, t: short_layer(where, t, 0, 16))
    psh[1, me] = row_of(sums[low, :])
    sent_s1_low = exchange(psh.at[1], 2)
    spectra(w2, taps, h2, ROWS)

    def gate_medium(where, rows, column):
        value = (
            pre[1, rows, where].astype(F32)
            * x1[rows, where].astype(F32)
            * twice(column)
            * gains[1:2, where]
        )
        a1[pl.ds(rows.start + HALF, HALF), where] = value.astype(BF16)

    def medium_layer(where, rows):
        window = a1[pl.ds(rows.start, ROWS), where]
        conv = filtered(w1, v1[HALF:, :], window, h1[:, where], False)
        value = (
            x1[rows, where].astype(F32) + post[1, rows, where].astype(F32) * conv
        ).astype(BF16)
        x2[rows, where] = value
        value = value.astype(F32)
        sums[rows, :] += fold(value * value)

    s1_high = inverse(collect(sent_s1_high, psh.at[0]))
    col_s[1, high] = col_of(s1_high)
    medium_halo = []
    for q in range(chunks):
        gate_medium(part(q), high, col_s[1, high])
        medium_halo.append(
            halo(a1.at[pl.ds(ROWS, HALF), part(q)], a1.at[pl.ds(0, HALF), part(q)], 2 + q, following)
        )

    local_part(e2, True)
    back_three = scan_three(back_two, r1_b, r2_b, o3_b, r3_b, 0, True)
    s1_low = inverse(collect(sent_s1_low, psh.at[1]))
    col_s[1, low] = col_of(s1_low)
    over_chunks(lambda where: gate_medium(where, low, col_s[1, low]))
    clear(low)
    clear(high)
    over_chunks(lambda where: medium_layer(where, high))
    finish(back_three)

    def back_long(rows, where, value):
        spread = (local[rows, where] + value).astype(BF16).astype(F32)
        u2[rows, where] = spread * pre[2, rows, where].astype(F32) * gains[2:3, where]

    carried(r3_b, True, back_long)

    def inner_sums(where, rows):
        sums2[rows, :] += x2[rows, where].astype(F32) * u2[rows, where]

    over_tiles(lambda where, t: inner_sums(where, high))
    ps2[0, me] = jnp.concatenate([row_of(sums[high, :]), row_of(sums2[high, :])], axis=0)
    sent_s2_high = exchange(ps2.at[0], 3)

    for q in range(chunks):
        medium_halo[q].wait_recv()

        @pl.when(k == 0)
        def _(q=q):
            a1[0:HALF, part(q)] = jnp.zeros((HALF, WIDE), BF16)

        medium_layer(part(q), low)
        sums2[low, :] += fold(x2[low, part(q)].astype(F32) * u2[low, part(q)])
    ps2[1, me] = jnp.concatenate([row_of(sums[low, :]), row_of(sums2[low, :])], axis=0)
    sent_s2_low = exchange(ps2.at[1], 4)

    def second_columns(sent, slots, rows):
        total = collect(sent, slots)
        s2 = inverse(total[0:1])
        col_s[2, rows] = col_of(s2)
        col_k[rows, :] = col_of(s2 * s2 * s2 * total[1:2] * (1.0 / channels))

    def back_two_rows(where, rows):
        value = (
            cot[rows, where].astype(F32)
            + u2[rows, where] * twice(col_s[2, rows])
            - x2[rows, where].astype(F32) * twice(col_k[rows, :])
        ).astype(BF16)
        g2[rows, where] = value
        e1[rows, where] = (post[1, rows, where].astype(F32) * value.astype(F32)).astype(BF16)

    second_columns(sent_s2_low, ps2.at[1], low)
    medium_back = []
    for q in range(chunks):
        back_two_rows(part(q), low)
        medium_back.append(
            halo(e1.at[pl.ds(0, HALF), part(q)], e1.at[pl.ds(ROWS, HALF), part(q)], 6 + q, preceding)
        )
    second_columns(sent_s2_high, ps2.at[0], high)
    over_chunks(lambda where: back_two_rows(where, high))

    def gate_long(where, t):
        value = (
            pre[2, :, where].astype(F32)
            * x2[:, where].astype(F32)
            * col_s[2]
            * gains[2:3, where]
        )
        a2[:, where] = value.astype(BF16)

    over_tiles(gate_long)
    states(a2, st_f, False)
    fore_one = scan_one(st_f, r1_f, 1)

    clear(low)
    clear(high)

    def medium_adjoint(where, rows):
        window = e1[pl.ds(rows.start, ROWS), where]
        spread = filtered(w1, v1[:HALF, :], window, h1[:, where], True)
        value = spread * pre[1, rows, where].astype(F32) * gains[1:2, where]
        u1[rows, where] = value
        sums[rows, :] += fold(value * x1[rows, where].astype(F32))

    over_chunks(lambda where: medium_adjoint(where, low))
    psh[2, me] = row_of(sums[low, :])
    sent_m1_low = exchange(psh.at[2], 5)
    local_part(a2, False)
    fore_two = scan_two(fore_one, r1_f, tz_f, r2_f, 1, False)

    def back_one_rows(where, t, rows):
        value = (
            g2[rows, where].astype(F32)
            + u1[rows, where] * col_s[1, rows, :]
            - x1[rows, where].astype(F32) * col_k[rows, :]
        ).astype(BF16)
        g1[rows, where] = value
        e0[t, rows, :] = (
            (post[0, rows, where].astype(F32) * value.astype(F32)).astype(BF16).astype(F32)
        )

    def short_adjoint(where, t, first, count):
        spread = se[0:1, where] * e0[t, pl.ds(first, count), :]
        for j in range(1, 7):
            spread += se[j : j + 1, where] * e0[t, pl.ds(first + j, count), :]
        rows = slice(first, first + count)
        value = spread * pre[0, rows, where].astype(F32) * gains[0:1, where]
        u0[rows, where] = value
        sums2[rows, :] += value * x0[rows, where].astype(F32)

    total = collect(sent_m1_low, psh.at[2])
    col_k[low, :] = col_of(s1_low * s1_low * s1_low * total * (1.0 / channels))
    over_tiles(lambda where, t: back_one_rows(where, t, low))
    short_back = halo(e0.at[:, pl.ds(0, 8), :], e0.at[:, pl.ds(256, 8), :], 1, preceding)
    over_tiles(lambda where, t: short_adjoint(where, t, 0, 112))

    for q in range(chunks):
        medium_back[q].wait_recv()

        @pl.when(k == kn - 1)
        def _(q=q):
            e1[ROWS : ROWS + HALF, part(q)] = jnp.zeros((HALF, WIDE), BF16)

        medium_adjoint(part(q), high)
    psh[3, me] = row_of(sums[high, :])
    sent_m1_high = exchange(psh.at[3], 6)
    fore_three = scan_three(fore_two, r1_f, r2_f, o3_f, r3_f, 1, False)
    short_back.wait_recv()

    @pl.when(k == kn - 1)
    def _():
        e0[:, 256:264, :] = jnp.zeros((tiles, 8, LANE), F32)

    total = collect(sent_m1_high, psh.at[3])
    col_k[high, :] = col_of(s1_high * s1_high * s1_high * total * (1.0 / channels))
    over_tiles(lambda where, t: back_one_rows(where, t, high))
    over_tiles(lambda where, t: short_adjoint(where, t, 112, 144))
    ps0[1, me] = row_of(sums2[...])
    sent_m0 = exchange(ps0.at[1], 7)

    finish(fore_three)

    def fore_long(rows, where, value):
        conv = (local[rows, where] + value).astype(BF16).astype(F32)
        result = x2[rows, where].astype(F32) + post[2, rows, where].astype(F32) * conv
        out[rows, where] = result.astype(BF16)

    carried(r3_f, False, fore_long)
    store_out = pltpu.make_async_copy(out, out_h, store_sem.at[1])
    store_out.start()

    total = collect(sent_m0, ps0.at[1])
    col_k[...] = col_of(s0 * s0 * s0 * total * (1.0 / channels))

    def final_rows(where, t):
        value = (
            g1[:, where].astype(F32)
            + u0[:, where] * col_s[0]
            - x0[:, where].astype(F32) * col_k[...]
        )
        grad[:, where] = value.astype(BF16)

    over_tiles(final_rows)
    store_grad = pltpu.make_async_copy(grad, grad_h, store_sem.at[0])
    store_grad.start()
    for copy in leaving:
        copy.wait_send()
    for copy, sends, gets in back_two + fore_two:

        @pl.when(sends)
        def _(copy=copy):
            copy.wait_send()

    store_out.wait()
    store_grad.wait()


def per_device(zn, tn, *args):
    stream, pre, post, gains, se, mr, res, dec, cot = args
    width = stream.shape[1]
    channels = width * tn
    tiles = width // LANE
    tables = (
        jnp.asarray(dft_matrix(WIDE, WIDE), BF16),
        jnp.asarray(dft_matrix(WIDE, WIDE).T * (2.0 / WIDE), BF16),
        jnp.asarray(dft_matrix(2 * ROWS, ROWS), BF16),
        jnp.asarray(dft_matrix(2 * ROWS, ROWS).T * (1.0 / ROWS), BF16),
    )
    operands = (stream, pre, post, gains, se, mr, res.T, dec.T, cot) + tables
    vmem = pltpu.VMEM
    whole = (ROWS, width)
    scan = (YN, POLES, WIDE)
    scratch = [vmem(o.shape, o.dtype) for o in operands]
    scratch += [
        vmem(whole, BF16),
        vmem(whole, BF16),
        vmem((tiles, ROWS + 8, LANE), F32),
        vmem((tiles, ROWS + 8, LANE), F32),
        vmem((ROWS + HALF, width), BF16),
        vmem((ROWS + HALF, width), BF16),
        vmem(whole, BF16),
        vmem(whole, BF16),
        vmem(whole, F32),
        vmem(whole, F32),
        vmem(whole, F32),
        vmem(whole, BF16),
        vmem(whole, BF16),
        vmem(whole, F32),
        vmem(whole, BF16),
        vmem(whole, BF16),
        vmem((POLES, width), F32),
        vmem((POLES, 8, width), F32),
        vmem((POLES, 8, width), F32),
        vmem(whole, F32),
        vmem((WIDE, width), F32),
        vmem((2 * ROWS, width), F32),
        vmem((ROWS, LANE), F32),
        vmem((ROWS, LANE), F32),
        vmem((3, ROWS, LANE), F32),
        vmem((ROWS, LANE), F32),
        vmem((2, tn, 1, ROWS), F32),
        vmem((4, tn, 1, HALF), F32),
        vmem((2, tn, 2, HALF), F32),
        vmem(scan, F32), vmem(scan, F32),
        vmem(scan, F32), vmem(scan, F32),
        vmem(scan[1:], F32), vmem(scan[1:], F32),
        vmem((zn, POLES, WIDE), F32), vmem((zn, POLES, WIDE), F32),
        vmem(scan, F32), vmem(scan, F32),
        vmem(scan, F32), vmem(scan, F32),
    ]
    sem = pltpu.SemaphoreType.DMA
    scratch += [
        sem((17,)), sem((2,)), sem((8, tn)), sem((8, tn)), sem((10,)), sem((10,)),
        sem((2, YN)), sem((2, YN)), sem((2, zn)), sem((2, zn)), sem((2, YN)), sem((2, YN)),
    ]
    any_spec = pl.BlockSpec(memory_space=pl.ANY)
    return pl.pallas_call(
        functools.partial(kernel, zn, tn, channels),
        out_shape=(jax.ShapeDtypeStruct(whole, BF16), jax.ShapeDtypeStruct(whole, BF16)),
        in_specs=[any_spec] * len(operands),
        out_specs=(any_spec, any_spec),
        scratch_shapes=scratch,
        compiler_params=pltpu.CompilerParams(
            collective_id=0, has_side_effects=True, vmem_limit_bytes=60 * 2**20
        ),
        cost_estimate=pl.CostEstimate(
            flops=4_000_000_000, bytes_accessed=7_000_000, transcendentals=500_000
        ),
        name="hyena_group",
    )(*operands)


def solution(mesh):
    zn = mesh.shape["context"] // YN
    tn = mesh.shape["tensor"]
    placed = (
        P("context", "tensor"),
        P(None, "context", "tensor"),
        P(None, "context", "tensor"),
        P(None, "tensor"),
        P(None, "tensor"),
        P(None, "tensor"),
        P("tensor", None),
        P("tensor", None),
        P("context", "tensor"),
    )
    return jax.shard_map(
        functools.partial(per_device, zn, tn),
        mesh=mesh,
        in_specs=placed,
        out_specs=(P("context", "tensor"), P("context", "tensor")),
        check_vma=False,
    )
```

```python
import functools
import math

import jax
import jax.numpy as jnp
import numpy as np
from jax import lax
from jax.experimental import pallas as pl
from jax.experimental.pallas import tpu as pltpu
from jax.sharding import PartitionSpec as P

EPSILON = 1e-06
F32 = jnp.float32
BF16 = jnp.bfloat16
MESH = pl.DeviceIdType.MESH
ROWS = 256
HALF = 128
LANE = 128
WIDE = 256
POLES = 16
YN = 4


def dft_matrix(points, used):
    freqs = (2 * np.arange(points // 2)[:, None] + 1) * np.arange(used)[None, :] % (2 * points)
    angle = freqs * (math.pi / points)
    return np.concatenate([np.cos(angle), -np.sin(angle)], axis=0)


def lanes(index, width=LANE):
    return pl.ds(pl.multiple_of(index * width, width), width)


def dot(a, b):
    return jnp.dot(a, b, preferred_element_type=F32)


def split(value):
    high = value.astype(BF16)
    return high, (value - high.astype(F32)).astype(BF16)


def kernel(
    zn,
    tn,
    channels,
    stream_h, pre_h, post_h, gains_h, se_h, mr_h, res_h, dec_h, cot_h, w1_h, v1_h, w2_h, v2_h,
    both_h,
    x0, pre, post, gains, se, mr, res, dect, cot, w1, v1, w2, v2,
    x1, x2, a0, e0, a1, e1, e2, a2, u0, u1, u2, g1, g2, local, out, grad,
    weight, decb, pow8, taps, h1, h2,
    ahead, x1h, s1r, col_h, sums, sums2, col_s, col_k, ps0, psh, ps2,
    st_b, st_f, r1_b, r1_f, tz_b, tz_f, r2_b, r2_f, o3_b, o3_f, r3_b, r3_f,
    load_sem, store_sem, ps_send, ps_recv, halo_send, halo_recv,
    sc1_send, sc1_recv, sc2_send, sc2_recv, sc3_send, sc3_recv,
):
    k = lax.axis_index("context")
    me = lax.axis_index("tensor")
    kn = zn * YN
    z = k // YN
    y = k % YN
    width = x0.shape[1]
    tiles = width // LANE
    chunks = width // WIDE
    following = (k + 1) % kn
    preceding = (k + kn - 1) % kn

    plan = [
        (stream_h, x0), (dec_h, dect), (res_h, res), (cot_h, cot), (post_h.at[2], post.at[2]),
        (w1_h, w1), (mr_h, mr), (gains_h, gains), (se_h, se), (w2_h, w2), (v2_h, v2), (v1_h, v1),
        (pre_h.at[0], pre.at[0]), (post_h.at[0], post.at[0]), (pre_h.at[1], pre.at[1]),
        (post_h.at[1], post.at[1]), (pre_h.at[2], pre.at[2]),
    ]
    loads = [pltpu.make_async_copy(s, d, load_sem.at[i]) for i, (s, d) in enumerate(plan)]
    for load in loads:
        load.start()

    r2_b[...] = jnp.zeros_like(r2_b)
    r2_f[...] = jnp.zeros_like(r2_f)

    barrier = pltpu.get_barrier_semaphore()
    partners = [{"tensor": (me + d) % tn} for d in range(1, tn)]
    partners += [{"context": z * YN + (y + d) % YN} for d in range(1, YN)]
    partners += [{"context": ((z + d) % zn) * YN + y} for d in range(1, zn)]
    partners += [{"context": following}, {"context": preceding}]
    for partner in partners:
        pl.semaphore_signal(barrier, inc=1, device_id=partner, device_id_type=MESH)

    def row_of(total):
        return jnp.sum(total.T, axis=0, keepdims=True)

    def col_of(row):
        return jnp.broadcast_to(row, (LANE, row.shape[1])).T

    leaving = []

    def exchange(slots, phase):
        sent = []
        for d in range(1, tn):
            sent.append(
                pltpu.make_async_remote_copy(
                    src_ref=slots.at[me],
                    dst_ref=slots.at[me],
                    send_sem=ps_send.at[phase, d],
                    recv_sem=ps_recv.at[phase, d],
                    device_id={"tensor": (me + d) % tn},
                    device_id_type=MESH,
                )
            )
        for copy in sent:
            copy.start()
        leaving.extend(sent)
        return sent

    def collect(sent, slots):
        for copy in sent:
            copy.wait_recv()
        total = slots[0]
        for index in range(1, tn):
            total = total + slots[index]
        return total

    def halo(src, dst, index, target):
        copy = pltpu.make_async_remote_copy(
            src_ref=src,
            dst_ref=dst,
            send_sem=halo_send.at[index],
            recv_sem=halo_recv.at[index],
            device_id={"context": target},
            device_id_type=MESH,
        )
        copy.start()
        leaving.append(copy)
        return copy

    def pole_tables():
        rate = dect[...]
        square = rate * rate
        series = rate * (
            1.0 + square * (1.0 / 6.0) * (1.0 + square * (1.0 / 20.0) * (1.0 + square * (1.0 / 42.0)))
        )
        weight[...] = res[...] * jnp.sqrt(2.0 * jnp.exp(-rate) * series)
        for r in range(POLES):
            wide = jnp.broadcast_to(dect[r : r + 1, :], (8, width))
            decb[r] = wide
            pow8[r] = jnp.exp(-8.0 * wide)

    def sublane():
        return lax.broadcasted_iota(jnp.int32, (1, 8, LANE), 1).astype(F32)

    def states(src, dst, reverse):
        def quarter(q, carry):
            for side in range(2):
                where = lanes(q * 2 + side)
                base = pow8[:, :, where]
                total = jnp.zeros((POLES, 8, LANE), F32)

                def step(g, total):
                    group = (ROWS // 16 - 1 - g) if reverse else g
                    rows = pl.ds(pl.multiple_of(group * 16, 16), 16)
                    value = src[rows, where].astype(F32)
                    first, second = (value[8:], value[:8]) if reverse else (value[:8], value[8:])
                    total = total * base + first[None]
                    return total * base + second[None]

                total = lax.fori_loop(0, ROWS // 16, step, total, unroll=True)
                place = sublane() if reverse else 7.0 - sublane()
                total = total * jnp.exp(-decb[:, :, where] * place)
                dst[q, :, side * LANE : (side + 1) * LANE] = jnp.sum(total, axis=1)
            return carry

        lax.fori_loop(0, chunks, quarter, 0)

    def spread_poles(start, base, reverse, sink):
        def step(g, state):
            group = (ROWS // 16 - 1 - g) if reverse else g
            rows = pl.ds(pl.multiple_of(group * 16, 16), 16)
            first = jnp.sum(state, axis=0)
            state = state * base
            second = jnp.sum(state, axis=0)
            state = state * base
            pair = [second, first] if reverse else [first, second]
            sink(rows, jnp.concatenate(pair, axis=0))
            return state

        lax.fori_loop(0, ROWS // 16, step, start, unroll=True)

    def stacked(ref, index, where):
        return jnp.stack(
            [jnp.broadcast_to(ref[index, r : r + 1, where], (8, LANE)) for r in range(POLES)]
        )

    def stacked_flat(ref, where):
        return jnp.stack(
            [jnp.broadcast_to(ref[r : r + 1, where], (8, LANE)) for r in range(POLES)]
        )

    def filter_head():
        def tile(t, carry):
            where = lanes(t)
            start = stacked_flat(weight, where) * jnp.exp(-decb[:, :, where] * sublane())

            def sink(rows, value):
                taps[rows, where] = value

            spread_poles(start, pow8[:, :, where], False, sink)
            return carry

        lax.fori_loop(0, tiles, tile, 0)

    def spectra(matrix, source, dst, used):
        def chunk(q, carry):
            where = lanes(q, WIDE)
            high, low = split(source[:, where])
            table = matrix[:, :used]
            dst[:, where] = dot(
                jnp.concatenate([table, table], axis=1), jnp.concatenate([high, low], axis=0)
            )
            return carry

        lax.fori_loop(0, chunks, chunk, 0, unroll=True)

    def filtered(matrix, back, window, spectrum, adjoint):
        half = matrix.shape[0] // 2
        image = dot(matrix[...], window)
        re, im = image[:half], image[half:]
        hre, him = spectrum[:half], spectrum[half:]
        if adjoint:
            out_re = re * hre + im * him
            out_im = im * hre - re * him
        else:
            out_re = re * hre - im * him
            out_im = re * him + im * hre
        product = jnp.concatenate([out_re.astype(BF16), out_im.astype(BF16)], axis=0)
        return dot(back, product)

    def local_part(src, adjoint):
        def chunk(q, carry):
            where = lanes(q, WIDE)
            local[:, where] = filtered(w2, v2[...], src[:, where], h2[:, where], adjoint)
            return carry

        lax.fori_loop(0, chunks, chunk, 0, unroll=True)

    def scan_one(st, r1, line):
        sent = []
        for d in range(1, YN):
            other = (y + d) % YN
            sent.append(
                pltpu.make_async_remote_copy(
                    src_ref=st.at[other],
                    dst_ref=r1.at[y],
                    send_sem=sc1_send.at[line, d],
                    recv_sem=sc1_recv.at[line, d],
                    device_id={"context": z * YN + other},
                    device_id_type=MESH,
                )
            )
        for copy in sent:
            copy.start()
        leaving.extend(sent)
        r1[y] = st[y]
        return sent

    def finish(sent):
        for copy in sent:
            copy.wait_recv()

    def rate_here():
        return dect[:, lanes(y, WIDE)]

    def scan_two(sent, r1, tz, r2, line, reverse):
        finish(sent)
        step = jnp.exp(-float(ROWS) * rate_here())
        order = range(YN - 1, -1, -1) if reverse else range(YN)
        total = jnp.zeros((POLES, WIDE), F32)
        for index in order:
            total = total * step + r1[index]
        tz[...] = total
        moved = []
        for d in range(1, zn):
            target = z - d if reverse else z + d
            source = z + d if reverse else z - d
            copy = pltpu.make_async_remote_copy(
                src_ref=tz,
                dst_ref=r2.at[z],
                send_sem=sc2_send.at[line, d],
                recv_sem=sc2_recv.at[line, d],
                device_id={"context": ((target + zn) % zn) * YN + y},
                device_id_type=MESH,
            )
            sends = (target >= 0) if reverse else (target < zn)
            gets = (source < zn) if reverse else (source >= 0)

            @pl.when(sends)
            def _(copy=copy):
                copy.start()

            moved.append((copy, sends, gets))
        return moved

    def scan_three(moved, r1, r2, o3, r3, line, reverse):
        for copy, sends, gets in moved:

            @pl.when(gets)
            def _(copy=copy):
                copy.wait_recv()

        rate = rate_here()
        step = jnp.exp(-float(ROWS) * rate)
        group = jnp.exp(-float(ROWS * YN) * rate)
        state = jnp.zeros((POLES, WIDE), F32)
        for d in range(zn - 1, 0, -1):
            source = (z + d) if reverse else (z - d)
            state = state * group + r2[(source + zn) % zn]
        order = range(YN - 1, -1, -1) if reverse else range(YN)
        for index in order:
            o3[index] = state
            state = state * step + r1[index]
        sent = []
        for d in range(1, YN):
            other = (y + d) % YN
            sent.append(
                pltpu.make_async_remote_copy(
                    src_ref=o3.at[other],
                    dst_ref=r3.at[y],
                    send_sem=sc3_send.at[line, d],
                    recv_sem=sc3_recv.at[line, d],
                    device_id={"context": z * YN + other},
                    device_id_type=MESH,
                )
            )
        for copy in sent:
            copy.start()
        leaving.extend(sent)
        r3[y] = o3[y]
        return sent

    def carried(r3, reverse, sink):
        def quarter(q, carry):
            for side in range(2):
                where = lanes(q * 2 + side)
                inner = slice(side * LANE, (side + 1) * LANE)
                place = (8.0 - sublane()) if reverse else (sublane() + 1.0)
                start = (
                    stacked(r3, q, inner)
                    * stacked_flat(weight, where)
                    * jnp.exp(-decb[:, :, where] * place)
                )
                spread_poles(
                    start, pow8[:, :, where], reverse, lambda rows, value: sink(rows, where, value)
                )
            return carry

        lax.fori_loop(0, chunks, quarter, 0)

    def over_tiles(body):
        def step(t, carry):
            body(lanes(t), t)
            return carry

        lax.fori_loop(0, tiles, step, 0)

    def over_chunks(body):
        def step(q, carry):
            body(lanes(q, WIDE))
            return carry

        lax.fori_loop(0, chunks, step, 0, unroll=True)

    def fold(value):
        return sum(value[:, i * LANE : (i + 1) * LANE] for i in range(value.shape[1] // LANE))

    def twice(column):
        return jnp.concatenate([column] * (WIDE // LANE), axis=1)

    low = slice(0, HALF)
    high = slice(HALF, ROWS)

    def inverse(total):
        return lax.rsqrt(total * (1.0 / channels) + EPSILON)

    def clear(rows):
        sums[rows, :] = jnp.zeros((HALF, LANE), F32)
        sums2[rows, :] = jnp.zeros((HALF, LANE), F32)

    def part(q):
        return slice(q * WIDE, (q + 1) * WIDE)

    loads[0].wait()
    clear(low)
    clear(high)

    def square_stream(where, t):
        value = x0[:, where].astype(F32)
        sums[...] += value * value

    over_tiles(square_stream)
    ps0[0, me] = row_of(sums[...])

    for load in loads[1:5]:
        load.wait()
    pole_tables()

    def cotangent_gate(where, t):
        e2[:, where] = (post[2, :, where].astype(F32) * cot[:, where].astype(F32)).astype(BF16)

    over_tiles(cotangent_gate)
    states(e2, st_b, True)

    pl.semaphore_wait(barrier, len(partners))
    sent_s0 = exchange(ps0.at[0], 0)

    back_one = scan_one(st_b, r1_b, 0)
    for load in loads[5:]:
        load.wait()
    filter_head()
    spectra(w1, mr, h1, HALF)
    spectra(w2, taps, h2, ROWS)
    back_two = scan_two(back_one, r1_b, tz_b, r2_b, 0, True)

    s0 = inverse(collect(sent_s0, ps0.at[0]))
    col_s[0] = col_of(s0)

    def gate_stream(where, t, first, count):
        rows = slice(first, first + count)
        value = (
            pre[0, rows, where].astype(F32)
            * x0[rows, where].astype(F32)
            * col_s[0, rows, :]
            * gains[0:1, where]
        )
        a0[t, pl.ds(first + 8, count), :] = value.astype(BF16).astype(F32)

    def short_layer(where, t, first, count):
        conv = se[0:1, where] * a0[t, pl.ds(first + 8, count), :]
        for j in range(1, 7):
            conv += se[j : j + 1, where] * a0[t, pl.ds(first + 8 - j, count), :]
        rows = slice(first, first + count)
        value = (x0[rows, where].astype(F32) + post[0, rows, where].astype(F32) * conv).astype(BF16)
        x1[rows, where] = value
        value = value.astype(F32)
        sums[rows, :] += value * value

    over_tiles(lambda where, t: gate_stream(where, t, 240, 16))
    short_halo = halo(a0.at[:, pl.ds(256, 8), :], a0.at[:, pl.ds(0, 8), :], 0, following)
    over_tiles(lambda where, t: gate_stream(where, t, 112, 128))
    clear(low)
    clear(high)
    stream_ahead = []
    for q in range(chunks):
        for t in range(q * WIDE // LANE, (q + 1) * WIDE // LANE):
            short_layer(slice(t * LANE, (t + 1) * LANE), t, 128, 128)
        gated = (
            pre[1, high, part(q)].astype(F32)
            * x1[high, part(q)].astype(F32)
            * gains[1:2, part(q)]
        )
        ahead[:, part(q)] = gated.astype(BF16)
        stream_ahead.append(halo(ahead.at[:, part(q)], x1h.at[:, part(q)], 2 + q, following))
    psh[0, me] = row_of(sums[high, :])
    sent_s1_high = exchange(psh.at[0], 1)

    over_tiles(lambda where, t: gate_stream(where, t, 0, 112))
    over_tiles(lambda where, t: short_layer(where, t, 16, 112))
    short_halo.wait_recv()

    @pl.when(k == 0)
    def _():
        a0[:, 0:8, :] = jnp.zeros((tiles, 8, LANE), F32)

    over_tiles(lambda where, t: short_layer(where, t, 0, 16))
    psh[1, me] = row_of(sums[low, :])
    sent_s1_low = exchange(psh.at[1], 2)
    local_part(e2, True)

    def gate_medium(where, rows, column):
        value = (
            pre[1, rows, where].astype(F32)
            * x1[rows, where].astype(F32)
            * twice(column)
            * gains[1:2, where]
        )
        a1[pl.ds(rows.start + HALF, HALF), where] = value.astype(BF16)

    def medium_layer(where, rows):
        window = a1[pl.ds(rows.start, ROWS), where]
        conv = filtered(w1, v1[HALF:, :], window, h1[:, where], False)
        value = (
            x1[rows, where].astype(F32) + post[1, rows, where].astype(F32) * conv
        ).astype(BF16)
        x2[rows, where] = value
        value = value.astype(F32)
        sums[rows, :] += fold(value * value)

    s1_high = inverse(collect(sent_s1_high, psh.at[0]))
    col_s[1, high] = col_of(s1_high)
    s1r[0] = s1_high
    scale_ahead = halo(s1r.at[0], s1r.at[1], 10, following)
    over_chunks(lambda where: gate_medium(where, high, col_s[1, high]))
    back_three = scan_three(back_two, r1_b, r2_b, o3_b, r3_b, 0, True)

    s1_low = inverse(collect(sent_s1_low, psh.at[1]))
    col_s[1, low] = col_of(s1_low)
    over_chunks(lambda where: gate_medium(where, low, col_s[1, low]))
    clear(low)
    clear(high)
    over_chunks(lambda where: medium_layer(where, high))
    scale_ahead.wait_recv()
    col_h[...] = col_of(s1r[1])
    for q in range(chunks):
        stream_ahead[q].wait_recv()
        value = x1h[:, part(q)].astype(F32) * twice(col_h[...])
        a1[0:HALF, part(q)] = value.astype(BF16)

        @pl.when(k == 0)
        def _(q=q):
            a1[0:HALF, part(q)] = jnp.zeros((HALF, WIDE), BF16)

        medium_layer(part(q), low)
    finish(back_three)

    def back_long(rows, where, value):
        spread = (local[rows, where] + value).astype(BF16).astype(F32)
        spread = spread * pre[2, rows, where].astype(F32) * gains[2:3, where]
        u2[rows, where] = spread
        sums2[rows, :] += x2[rows, where].astype(F32) * spread

    carried(r3_b, True, back_long)
    ps2[0, me] = jnp.concatenate([row_of(sums[low, :]), row_of(sums2[low, :])], axis=0)
    sent_s2_low = exchange(ps2.at[0], 3)
    ps2[1, me] = jnp.concatenate([row_of(sums[high, :]), row_of(sums2[high, :])], axis=0)
    sent_s2_high = exchange(ps2.at[1], 4)

    def second_columns(sent, slots, rows):
        total = collect(sent, slots)
        s2 = inverse(total[0:1])
        col_s[2, rows] = col_of(s2)
        col_k[rows, :] = col_of(s2 * s2 * s2 * total[1:2] * (1.0 / channels))

    def back_two_rows(where, rows):
        value = (
            cot[rows, where].astype(F32)
            + u2[rows, where] * twice(col_s[2, rows])
            - x2[rows, where].astype(F32) * twice(col_k[rows, :])
        ).astype(BF16)
        g2[rows, where] = value
        e1[rows, where] = (post[1, rows, where].astype(F32) * value.astype(F32)).astype(BF16)

    def gate_long(where, t):
        value = (
            pre[2, :, where].astype(F32)
            * x2[:, where].astype(F32)
            * col_s[2]
            * gains[2:3, where]
        )
        a2[:, where] = value.astype(BF16)

    second_columns(sent_s2_low, ps2.at[0], low)
    medium_back = []
    for q in range(chunks):
        back_two_rows(part(q), low)
        medium_back.append(
            halo(e1.at[pl.ds(0, HALF), part(q)], e1.at[pl.ds(ROWS, HALF), part(q)], 6 + q, preceding)
        )
        if q == 1:
            second_columns(sent_s2_high, ps2.at[1], high)
            over_tiles(gate_long)
            states(a2, st_f, False)
            fore_one = scan_one(st_f, r1_f, 1)
    over_chunks(lambda where: back_two_rows(where, high))

    clear(low)
    clear(high)

    def medium_adjoint(where, rows):
        window = e1[pl.ds(rows.start, ROWS), where]
        spread = filtered(w1, v1[:HALF, :], window, h1[:, where], True)
        value = spread * pre[1, rows, where].astype(F32) * gains[1:2, where]
        u1[rows, where] = value
        sums[rows, :] += fold(value * x1[rows, where].astype(F32))

    over_chunks(lambda where: medium_adjoint(where, low))
    psh[2, me] = row_of(sums[low, :])
    sent_m1_low = exchange(psh.at[2], 5)
    local_part(a2, False)
    fore_two = scan_two(fore_one, r1_f, tz_f, r2_f, 1, False)

    def back_one_rows(where, t, rows):
        value = (
            g2[rows, where].astype(F32)
            + u1[rows, where] * col_s[1, rows, :]
            - x1[rows, where].astype(F32) * col_k[rows, :]
        ).astype(BF16)
        g1[rows, where] = value
        e0[t, rows, :] = (
            (post[0, rows, where].astype(F32) * value.astype(F32)).astype(BF16).astype(F32)
        )

    def short_adjoint(where, t, first, count):
        spread = se[0:1, where] * e0[t, pl.ds(first, count), :]
        for j in range(1, 7):
            spread += se[j : j + 1, where] * e0[t, pl.ds(first + j, count), :]
        rows = slice(first, first + count)
        value = spread * pre[0, rows, where].astype(F32) * gains[0:1, where]
        u0[rows, where] = value
        sums2[rows, :] += value * x0[rows, where].astype(F32)

    total = collect(sent_m1_low, psh.at[2])
    col_k[low, :] = col_of(s1_low * s1_low * s1_low * total * (1.0 / channels))
    over_tiles(lambda where, t: back_one_rows(where, t, low))
    short_back = halo(e0.at[:, pl.ds(0, 8), :], e0.at[:, pl.ds(256, 8), :], 1, preceding)
    over_tiles(lambda where, t: short_adjoint(where, t, 0, 112))

    for q in range(chunks):
        medium_back[q].wait_recv()

        @pl.when(k == kn - 1)
        def _(q=q):
            e1[ROWS : ROWS + HALF, part(q)] = jnp.zeros((HALF, WIDE), BF16)

        medium_adjoint(part(q), high)
    psh[3, me] = row_of(sums[high, :])
    sent_m1_high = exchange(psh.at[3], 6)
    fore_three = scan_three(fore_two, r1_f, r2_f, o3_f, r3_f, 1, False)
    short_back.wait_recv()

    @pl.when(k == kn - 1)
    def _():
        e0[:, 256:264, :] = jnp.zeros((tiles, 8, LANE), F32)

    total = collect(sent_m1_high, psh.at[3])
    col_k[high, :] = col_of(s1_high * s1_high * s1_high * total * (1.0 / channels))
    over_tiles(lambda where, t: back_one_rows(where, t, high))
    over_tiles(lambda where, t: short_adjoint(where, t, 112, 144))
    ps0[1, me] = row_of(sums2[...])
    sent_m0 = exchange(ps0.at[1], 7)

    finish(fore_three)

    def fore_long(rows, where, value):
        conv = (local[rows, where] + value).astype(BF16).astype(F32)
        result = x2[rows, where].astype(F32) + post[2, rows, where].astype(F32) * conv
        out[rows, where] = result.astype(BF16)

    carried(r3_f, False, fore_long)
    store_out = pltpu.make_async_copy(out, both_h.at[0], store_sem.at[1])
    store_out.start()

    total = collect(sent_m0, ps0.at[1])
    col_k[...] = col_of(s0 * s0 * s0 * total * (1.0 / channels))

    def final_rows(where, t):
        value = (
            g1[:, where].astype(F32)
            + u0[:, where] * col_s[0]
            - x0[:, where].astype(F32) * col_k[...]
        )
        grad[:, where] = value.astype(BF16)

    over_tiles(final_rows)
    store_grad = pltpu.make_async_copy(grad, both_h.at[1], store_sem.at[0])
    store_grad.start()
    for copy in leaving:
        copy.wait_send()
    for copy, sends, gets in back_two + fore_two:

        @pl.when(sends)
        def _(copy=copy):
            copy.wait_send()

    store_out.wait()
    store_grad.wait()


def per_device(zn, tn, *args):
    stream, pre, post, gains, se, mr, res, dec, cot = args
    width = stream.shape[1]
    channels = width * tn
    tiles = width // LANE
    tables = (
        jnp.asarray(dft_matrix(WIDE, WIDE), BF16),
        jnp.asarray(dft_matrix(WIDE, WIDE).T * (2.0 / WIDE), BF16),
        jnp.asarray(dft_matrix(2 * ROWS, ROWS), BF16),
        jnp.asarray(dft_matrix(2 * ROWS, ROWS).T * (1.0 / ROWS), BF16),
    )
    operands = (stream, pre, post, gains, se, mr, res.T, dec.T, cot) + tables
    vmem = pltpu.VMEM
    whole = (ROWS, width)
    scan = (YN, POLES, WIDE)
    scratch = [vmem(o.shape, o.dtype) for o in operands]
    scratch += [
        vmem(whole, BF16),
        vmem(whole, BF16),
        vmem((tiles, ROWS + 8, LANE), F32),
        vmem((tiles, ROWS + 8, LANE), F32),
        vmem((ROWS + HALF, width), BF16),
        vmem((ROWS + HALF, width), BF16),
        vmem(whole, BF16),
        vmem(whole, BF16),
        vmem(whole, F32),
        vmem(whole, F32),
        vmem(whole, F32),
        vmem(whole, BF16),
        vmem(whole, BF16),
        vmem(whole, F32),
        vmem(whole, BF16),
        vmem(whole, BF16),
        vmem((POLES, width), F32),
        vmem((POLES, 8, width), F32),
        vmem((POLES, 8, width), F32),
        vmem(whole, F32),
        vmem((WIDE, width), F32),
        vmem((2 * ROWS, width), F32),
        vmem((HALF, width), BF16),
        vmem((HALF, width), BF16),
        vmem((2, 1, HALF), F32),
        vmem((HALF, LANE), F32),
        vmem((ROWS, LANE), F32),
        vmem((ROWS, LANE), F32),
        vmem((3, ROWS, LANE), F32),
        vmem((ROWS, LANE), F32),
        vmem((2, tn, 1, ROWS), F32),
        vmem((4, tn, 1, HALF), F32),
        vmem((2, tn, 2, HALF), F32),
        vmem(scan, F32), vmem(scan, F32),
        vmem(scan, F32), vmem(scan, F32),
        vmem(scan[1:], F32), vmem(scan[1:], F32),
        vmem((zn, POLES, WIDE), F32), vmem((zn, POLES, WIDE), F32),
        vmem(scan, F32), vmem(scan, F32),
        vmem(scan, F32), vmem(scan, F32),
    ]
    sem = pltpu.SemaphoreType.DMA
    scratch += [
        sem((17,)), sem((2,)), sem((8, tn)), sem((8, tn)), sem((11,)), sem((11,)),
        sem((2, YN)), sem((2, YN)), sem((2, zn)), sem((2, zn)), sem((2, YN)), sem((2, YN)),
    ]
    any_spec = pl.BlockSpec(memory_space=pl.ANY)
    both = pl.pallas_call(
        functools.partial(kernel, zn, tn, channels),
        out_shape=jax.ShapeDtypeStruct((2,) + whole, BF16),
        in_specs=[any_spec] * len(operands),
        out_specs=any_spec,
        scratch_shapes=scratch,
        compiler_params=pltpu.CompilerParams(
            collective_id=0, has_side_effects=True, vmem_limit_bytes=60 * 2**20
        ),
        cost_estimate=pl.CostEstimate(
            flops=4_000_000_000, bytes_accessed=7_000_000, transcendentals=500_000
        ),
        name="hyena_group",
    )(*operands)
    return both[0], both[1]


def solution(mesh):
    zn = mesh.shape["context"] // YN
    tn = mesh.shape["tensor"]
    placed = (
        P("context", "tensor"),
        P(None, "context", "tensor"),
        P(None, "context", "tensor"),
        P(None, "tensor"),
        P(None, "tensor"),
        P(None, "tensor"),
        P("tensor", None),
        P("tensor", None),
        P("context", "tensor"),
    )
    return jax.shard_map(
        functools.partial(per_device, zn, tn),
        mesh=mesh,
        in_specs=placed,
        out_specs=(P("context", "tensor"), P("context", "tensor")),
        check_vma=False,
    )
```

```python
import functools
import math

import jax
import jax.numpy as jnp
import numpy as np
from jax import lax
from jax.experimental import pallas as pl
from jax.experimental.pallas import tpu as pltpu
from jax.sharding import PartitionSpec as P

EPSILON = 1e-06
F32 = jnp.float32
BF16 = jnp.bfloat16
MESH = pl.DeviceIdType.MESH
ROWS = 256
HALF = 128
LANE = 128
WIDE = 256
POLES = 16
YN = 4


def dft_matrix(points, used):
    freqs = (2 * np.arange(points // 2)[:, None] + 1) * np.arange(used)[None, :] % (2 * points)
    angle = freqs * (math.pi / points)
    return np.concatenate([np.cos(angle), -np.sin(angle)], axis=0)


def lanes(index, width=LANE):
    return pl.ds(pl.multiple_of(index * width, width), width)


def dot(a, b):
    return jnp.dot(a, b, preferred_element_type=F32)


def split(value):
    high = value.astype(BF16)
    return high, (value - high.astype(F32)).astype(BF16)


def kernel(
    zn,
    tn,
    channels,
    stream_h, pre_h, post_h, gains_h, se_h, mr_h, res_h, dec_h, cot_h, w1_h, v1_h, w2_h, v2_h,
    both_h,
    x0, pre, post, gains, se, mr, res, dect, cot, w1, v1, w2, v2,
    x1, x2, a0, e0, a1, e1, e2, a2, u0, u1, u2, g1, g2, local, out, grad,
    weight, decb, pow8, taps, h1, h2,
    ahead, x1h, s1r, col_h, sums, sums2, col_s, col_k, ps0, psh, ps2,
    st_b, st_f, r1_b, r1_f, tz_b, tz_f, r2_b, r2_f, o3_b, o3_f, r3_b, r3_f,
    load_sem, store_sem, ps_send, ps_recv, halo_send, halo_recv,
    sc1_send, sc1_recv, sc2_send, sc2_recv, sc3_send, sc3_recv,
):
    k = lax.axis_index("context")
    me = lax.axis_index("tensor")
    kn = zn * YN
    z = k // YN
    y = k % YN
    width = x0.shape[1]
    tiles = width // LANE
    chunks = width // WIDE
    following = (k + 1) % kn
    preceding = (k + kn - 1) % kn

    plan = [
        (stream_h, x0), (dec_h, dect), (res_h, res), (cot_h, cot), (post_h.at[2], post.at[2]),
        (w1_h, w1), (mr_h, mr), (gains_h, gains), (se_h, se), (w2_h, w2), (v2_h, v2), (v1_h, v1),
        (pre_h.at[0], pre.at[0]), (post_h.at[0], post.at[0]), (pre_h.at[1], pre.at[1]),
        (post_h.at[1], post.at[1]), (pre_h.at[2], pre.at[2]),
    ]
    loads = [pltpu.make_async_copy(s, d, load_sem.at[i]) for i, (s, d) in enumerate(plan)]
    for load in loads:
        load.start()

    r2_b[...] = jnp.zeros_like(r2_b)
    r2_f[...] = jnp.zeros_like(r2_f)

    barrier = pltpu.get_barrier_semaphore()
    partners = [{"tensor": (me + d) % tn} for d in range(1, tn)]
    partners += [{"context": z * YN + (y + d) % YN} for d in range(1, YN)]
    partners += [{"context": ((z + d) % zn) * YN + y} for d in range(1, zn)]
    partners += [{"context": following}, {"context": preceding}]
    for partner in partners:
        pl.semaphore_signal(barrier, inc=1, device_id=partner, device_id_type=MESH)

    def row_of(total):
        return jnp.sum(total.T, axis=0, keepdims=True)

    def col_of(row):
        return jnp.broadcast_to(row, (LANE, row.shape[1])).T

    leaving = []

    def exchange(slots, phase):
        sent = []
        for d in range(1, tn):
            sent.append(
                pltpu.make_async_remote_copy(
                    src_ref=slots.at[me],
                    dst_ref=slots.at[me],
                    send_sem=ps_send.at[phase, d],
                    recv_sem=ps_recv.at[phase, d],
                    device_id={"tensor": (me + d) % tn},
                    device_id_type=MESH,
                )
            )
        for copy in sent:
            copy.start()
        leaving.extend(sent)
        return sent

    def collect(sent, slots):
        for copy in sent:
            copy.wait_recv()
        total = slots[0]
        for index in range(1, tn):
            total = total + slots[index]
        return total

    def halo(src, dst, index, target):
        copy = pltpu.make_async_remote_copy(
            src_ref=src,
            dst_ref=dst,
            send_sem=halo_send.at[index],
            recv_sem=halo_recv.at[index],
            device_id={"context": target},
            device_id_type=MESH,
        )
        copy.start()
        leaving.append(copy)
        return copy

    def pole_tables():
        rate = dect[...]
        square = rate * rate
        series = rate * (
            1.0 + square * (1.0 / 6.0) * (1.0 + square * (1.0 / 20.0) * (1.0 + square * (1.0 / 42.0)))
        )
        weight[...] = res[...] * jnp.sqrt(2.0 * jnp.exp(-rate) * series)
        for r in range(POLES):
            wide = jnp.broadcast_to(dect[r : r + 1, :], (8, width))
            decb[r] = wide
            pow8[r] = jnp.exp(-8.0 * wide)

    def sublane():
        return lax.broadcasted_iota(jnp.int32, (1, 8, LANE), 1).astype(F32)

    def states(src, dst, reverse):
        def quarter(q, carry):
            for side in range(2):
                where = lanes(q * 2 + side)
                base = pow8[:, :, where]
                total = jnp.zeros((POLES, 8, LANE), F32)

                def step(g, total):
                    group = (ROWS // 16 - 1 - g) if reverse else g
                    rows = pl.ds(pl.multiple_of(group * 16, 16), 16)
                    value = src[rows, where].astype(F32)
                    first, second = (value[8:], value[:8]) if reverse else (value[:8], value[8:])
                    total = total * base + first[None]
                    return total * base + second[None]

                total = lax.fori_loop(0, ROWS // 16, step, total, unroll=True)
                place = sublane() if reverse else 7.0 - sublane()
                total = total * jnp.exp(-decb[:, :, where] * place)
                dst[q, :, side * LANE : (side + 1) * LANE] = jnp.sum(total, axis=1)
            return carry

        lax.fori_loop(0, chunks, quarter, 0)

    def spread_poles(start, base, reverse, sink):
        def step(g, state):
            group = (ROWS // 16 - 1 - g) if reverse else g
            rows = pl.ds(pl.multiple_of(group * 16, 16), 16)
            first = jnp.sum(state, axis=0)
            state = state * base
            second = jnp.sum(state, axis=0)
            state = state * base
            pair = [second, first] if reverse else [first, second]
            sink(rows, jnp.concatenate(pair, axis=0))
            return state

        lax.fori_loop(0, ROWS // 16, step, start, unroll=True)

    def stacked(ref, index, where):
        return jnp.stack(
            [jnp.broadcast_to(ref[index, r : r + 1, where], (8, LANE)) for r in range(POLES)]
        )

    def stacked_flat(ref, where):
        return jnp.stack(
            [jnp.broadcast_to(ref[r : r + 1, where], (8, LANE)) for r in range(POLES)]
        )

    def filter_head():
        def tile(t, carry):
            where = lanes(t)
            start = stacked_flat(weight, where) * jnp.exp(-decb[:, :, where] * sublane())

            def sink(rows, value):
                taps[rows, where] = value

            spread_poles(start, pow8[:, :, where], False, sink)
            return carry

        lax.fori_loop(0, tiles, tile, 0)

    def spectra(matrix, source, dst, used):
        def chunk(q, carry):
            where = lanes(q, WIDE)
            high, low = split(source[:, where])
            table = matrix[:, :used]
            dst[:, where] = dot(
                jnp.concatenate([table, table], axis=1), jnp.concatenate([high, low], axis=0)
            )
            return carry

        lax.fori_loop(0, chunks, chunk, 0, unroll=True)

    def filtered(matrix, back, window, spectrum, adjoint):
        half = matrix.shape[0] // 2
        image = dot(matrix[...], window)
        re, im = image[:half], image[half:]
        hre, him = spectrum[:half], spectrum[half:]
        if adjoint:
            out_re = re * hre + im * him
            out_im = im * hre - re * him
        else:
            out_re = re * hre - im * him
            out_im = re * him + im * hre
        product = jnp.concatenate([out_re.astype(BF16), out_im.astype(BF16)], axis=0)
        return dot(back, product)

    def local_part(src, adjoint):
        def chunk(q, carry):
            where = lanes(q, WIDE)
            local[:, where] = filtered(w2, v2[...], src[:, where], h2[:, where], adjoint)
            return carry

        lax.fori_loop(0, chunks, chunk, 0, unroll=True)

    def scan_one(st, r1, line):
        sent = []
        for d in range(1, YN):
            other = (y + d) % YN
            sent.append(
                pltpu.make_async_remote_copy(
                    src_ref=st.at[other],
                    dst_ref=r1.at[y],
                    send_sem=sc1_send.at[line, d],
                    recv_sem=sc1_recv.at[line, d],
                    device_id={"context": z * YN + other},
                    device_id_type=MESH,
                )
            )
        for copy in sent:
            copy.start()
        leaving.extend(sent)
        r1[y] = st[y]
        return sent

    def finish(sent):
        for copy in sent:
            copy.wait_recv()

    def rate_here():
        return dect[:, lanes(y, WIDE)]

    def scan_two(sent, r1, tz, r2, line, reverse):
        finish(sent)
        step = jnp.exp(-float(ROWS) * rate_here())
        order = range(YN - 1, -1, -1) if reverse else range(YN)
        total = jnp.zeros((POLES, WIDE), F32)
        for index in order:
            total = total * step + r1[index]
        tz[...] = total
        moved = []
        for d in range(1, zn):
            target = z - d if reverse else z + d
            source = z + d if reverse else z - d
            copy = pltpu.make_async_remote_copy(
                src_ref=tz,
                dst_ref=r2.at[z],
                send_sem=sc2_send.at[line, d],
                recv_sem=sc2_recv.at[line, d],
                device_id={"context": ((target + zn) % zn) * YN + y},
                device_id_type=MESH,
            )
            sends = (target >= 0) if reverse else (target < zn)
            gets = (source < zn) if reverse else (source >= 0)

            @pl.when(sends)
            def _(copy=copy):
                copy.start()

            moved.append((copy, sends, gets))
        return moved

    def scan_three(moved, r1, r2, o3, r3, line, reverse):
        for copy, sends, gets in moved:

            @pl.when(gets)
            def _(copy=copy):
                copy.wait_recv()

        rate = rate_here()
        step = jnp.exp(-float(ROWS) * rate)
        group = jnp.exp(-float(ROWS * YN) * rate)
        state = jnp.zeros((POLES, WIDE), F32)
        for d in range(zn - 1, 0, -1):
            source = (z + d) if reverse else (z - d)
            state = state * group + r2[(source + zn) % zn]
        order = range(YN - 1, -1, -1) if reverse else range(YN)
        for index in order:
            o3[index] = state
            state = state * step + r1[index]
        sent = []
        for d in range(1, YN):
            other = (y + d) % YN
            sent.append(
                pltpu.make_async_remote_copy(
                    src_ref=o3.at[other],
                    dst_ref=r3.at[y],
                    send_sem=sc3_send.at[line, d],
                    recv_sem=sc3_recv.at[line, d],
                    device_id={"context": z * YN + other},
                    device_id_type=MESH,
                )
            )
        for copy in sent:
            copy.start()
        leaving.extend(sent)
        r3[y] = o3[y]
        return sent

    def carried(r3, reverse, sink):
        def quarter(q, carry):
            for side in range(2):
                where = lanes(q * 2 + side)
                inner = slice(side * LANE, (side + 1) * LANE)
                place = (8.0 - sublane()) if reverse else (sublane() + 1.0)
                start = (
                    stacked(r3, q, inner)
                    * stacked_flat(weight, where)
                    * jnp.exp(-decb[:, :, where] * place)
                )
                spread_poles(
                    start, pow8[:, :, where], reverse, lambda rows, value: sink(rows, where, value)
                )
            return carry

        lax.fori_loop(0, chunks, quarter, 0)

    def over_tiles(body):
        def step(t, carry):
            body(lanes(t), t)
            return carry

        lax.fori_loop(0, tiles, step, 0)

    def over_chunks(body):
        def step(q, carry):
            body(lanes(q, WIDE))
            return carry

        lax.fori_loop(0, chunks, step, 0, unroll=True)

    def fold(value):
        return sum(value[:, i * LANE : (i + 1) * LANE] for i in range(value.shape[1] // LANE))

    def twice(column):
        return jnp.concatenate([column] * (WIDE // LANE), axis=1)

    low = slice(0, HALF)
    high = slice(HALF, ROWS)

    def inverse(total):
        return lax.rsqrt(total * (1.0 / channels) + EPSILON)

    def clear(rows):
        sums[rows, :] = jnp.zeros((HALF, LANE), F32)
        sums2[rows, :] = jnp.zeros((HALF, LANE), F32)

    def part(q):
        return slice(q * WIDE, (q + 1) * WIDE)

    loads[0].wait()
    clear(low)
    clear(high)

    def square_stream(where, t):
        value = x0[:, where].astype(F32)
        sums[...] += value * value

    over_tiles(square_stream)
    ps0[0, me] = row_of(sums[...])

    for load in loads[1:5]:
        load.wait()
    pole_tables()

    def cotangent_gate(where, t):
        e2[:, where] = (post[2, :, where].astype(F32) * cot[:, where].astype(F32)).astype(BF16)

    over_tiles(cotangent_gate)
    states(e2, st_b, True)

    pl.semaphore_wait(barrier, len(partners))
    sent_s0 = exchange(ps0.at[0], 0)

    back_one = scan_one(st_b, r1_b, 0)
    for load in loads[5:]:
        load.wait()
    spectra(w1, mr, h1, HALF)
    back_two = scan_two(back_one, r1_b, tz_b, r2_b, 0, True)

    s0 = inverse(collect(sent_s0, ps0.at[0]))
    col_s[0] = col_of(s0)

    def gate_stream(where, t, first, count):
        rows = slice(first, first + count)
        value = (
            pre[0, rows, where].astype(F32)
            * x0[rows, where].astype(F32)
            * col_s[0, rows, :]
            * gains[0:1, where]
        )
        a0[t, pl.ds(first + 8, count), :] = value.astype(BF16).astype(F32)

    def short_layer(where, t, first, count):
        conv = se[0:1, where] * a0[t, pl.ds(first + 8, count), :]
        for j in range(1, 7):
            conv += se[j : j + 1, where] * a0[t, pl.ds(first + 8 - j, count), :]
        rows = slice(first, first + count)
        value = (x0[rows, where].astype(F32) + post[0, rows, where].astype(F32) * conv).astype(BF16)
        x1[rows, where] = value
        value = value.astype(F32)
        sums[rows, :] += value * value

    over_tiles(lambda where, t: gate_stream(where, t, 240, 16))
    short_halo = halo(a0.at[:, pl.ds(256, 8), :], a0.at[:, pl.ds(0, 8), :], 0, following)
    over_tiles(lambda where, t: gate_stream(where, t, 112, 128))
    clear(low)
    clear(high)
    stream_ahead = []
    for q in range(chunks):
        for t in range(q * WIDE // LANE, (q + 1) * WIDE // LANE):
            short_layer(slice(t * LANE, (t + 1) * LANE), t, 128, 128)
        gated = (
            pre[1, high, part(q)].astype(F32)
            * x1[high, part(q)].astype(F32)
            * gains[1:2, part(q)]
        )
        ahead[:, part(q)] = gated.astype(BF16)
        stream_ahead.append(halo(ahead.at[:, part(q)], x1h.at[:, part(q)], 2 + q, following))
    psh[0, me] = row_of(sums[high, :])
    sent_s1_high = exchange(psh.at[0], 1)

    over_tiles(lambda where, t: gate_stream(where, t, 0, 112))
    over_tiles(lambda where, t: short_layer(where, t, 16, 112))
    filter_head()
    spectra(w2, taps, h2, ROWS)
    short_halo.wait_recv()

    @pl.when(k == 0)
    def _():
        a0[:, 0:8, :] = jnp.zeros((tiles, 8, LANE), F32)

    over_tiles(lambda where, t: short_layer(where, t, 0, 16))
    psh[1, me] = row_of(sums[low, :])
    sent_s1_low = exchange(psh.at[1], 2)
    local_part(e2, True)

    def gate_medium(where, rows, column):
        value = (
            pre[1, rows, where].astype(F32)
            * x1[rows, where].astype(F32)
            * twice(column)
            * gains[1:2, where]
        )
        a1[pl.ds(rows.start + HALF, HALF), where] = value.astype(BF16)

    def medium_layer(where, rows):
        window = a1[pl.ds(rows.start, ROWS), where]
        conv = filtered(w1, v1[HALF:, :], window, h1[:, where], False)
        value = (
            x1[rows, where].astype(F32) + post[1, rows, where].astype(F32) * conv
        ).astype(BF16)
        x2[rows, where] = value
        value = value.astype(F32)
        sums[rows, :] += fold(value * value)

    s1_high = inverse(collect(sent_s1_high, psh.at[0]))
    col_s[1, high] = col_of(s1_high)
    s1r[0] = s1_high
    scale_ahead = halo(s1r.at[0], s1r.at[1], 10, following)
    over_chunks(lambda where: gate_medium(where, high, col_s[1, high]))
    back_three = scan_three(back_two, r1_b, r2_b, o3_b, r3_b, 0, True)

    s1_low = inverse(collect(sent_s1_low, psh.at[1]))
    col_s[1, low] = col_of(s1_low)
    over_chunks(lambda where: gate_medium(where, low, col_s[1, low]))
    clear(low)
    clear(high)
    over_chunks(lambda where: medium_layer(where, high))
    scale_ahead.wait_recv()
    col_h[...] = col_of(s1r[1])
    for q in range(chunks):
        stream_ahead[q].wait_recv()
        value = x1h[:, part(q)].astype(F32) * twice(col_h[...])
        a1[0:HALF, part(q)] = value.astype(BF16)

        @pl.when(k == 0)
        def _(q=q):
            a1[0:HALF, part(q)] = jnp.zeros((HALF, WIDE), BF16)

        medium_layer(part(q), low)
    finish(back_three)

    def back_long(rows, where, value):
        spread = (local[rows, where] + value).astype(BF16).astype(F32)
        spread = spread * pre[2, rows, where].astype(F32) * gains[2:3, where]
        u2[rows, where] = spread
        sums2[rows, :] += x2[rows, where].astype(F32) * spread

    carried(r3_b, True, back_long)
    ps2[me] = jnp.concatenate([row_of(sums[...]), row_of(sums2[...])], axis=0)
    sent_s2 = exchange(ps2, 3)

    def back_two_rows(where, rows):
        value = (
            cot[rows, where].astype(F32)
            + u2[rows, where] * twice(col_s[2, rows])
            - x2[rows, where].astype(F32) * twice(col_k[rows, :])
        ).astype(BF16)
        g2[rows, where] = value
        e1[rows, where] = (post[1, rows, where].astype(F32) * value.astype(F32)).astype(BF16)

    def gate_long(where, t):
        value = (
            pre[2, :, where].astype(F32)
            * x2[:, where].astype(F32)
            * col_s[2]
            * gains[2:3, where]
        )
        a2[:, where] = value.astype(BF16)

    total = collect(sent_s2, ps2)
    s2 = inverse(total[0:1])
    col_s[2] = col_of(s2)
    col_k[...] = col_of(s2 * s2 * s2 * total[1:2] * (1.0 / channels))
    medium_back = []
    for q in range(chunks):
        back_two_rows(part(q), low)
        medium_back.append(
            halo(e1.at[pl.ds(0, HALF), part(q)], e1.at[pl.ds(ROWS, HALF), part(q)], 6 + q, preceding)
        )
        if q == 1:
            over_tiles(gate_long)
            states(a2, st_f, False)
            fore_one = scan_one(st_f, r1_f, 1)
    over_chunks(lambda where: back_two_rows(where, high))

    clear(low)
    clear(high)

    def medium_adjoint(where, rows):
        window = e1[pl.ds(rows.start, ROWS), where]
        spread = filtered(w1, v1[:HALF, :], window, h1[:, where], True)
        value = spread * pre[1, rows, where].astype(F32) * gains[1:2, where]
        u1[rows, where] = value
        sums[rows, :] += fold(value * x1[rows, where].astype(F32))

    over_chunks(lambda where: medium_adjoint(where, low))
    psh[2, me] = row_of(sums[low, :])
    sent_m1_low = exchange(psh.at[2], 5)
    fore_two = scan_two(fore_one, r1_f, tz_f, r2_f, 1, False)

    def back_one_rows(where, t, rows):
        value = (
            g2[rows, where].astype(F32)
            + u1[rows, where] * col_s[1, rows, :]
            - x1[rows, where].astype(F32) * col_k[rows, :]
        ).astype(BF16)
        g1[rows, where] = value
        e0[t, rows, :] = (
            (post[0, rows, where].astype(F32) * value.astype(F32)).astype(BF16).astype(F32)
        )

    def short_adjoint(where, t, first, count):
        spread = se[0:1, where] * e0[t, pl.ds(first, count), :]
        for j in range(1, 7):
            spread += se[j : j + 1, where] * e0[t, pl.ds(first + j, count), :]
        rows = slice(first, first + count)
        value = spread * pre[0, rows, where].astype(F32) * gains[0:1, where]
        u0[rows, where] = value
        sums2[rows, :] += value * x0[rows, where].astype(F32)

    total = collect(sent_m1_low, psh.at[2])
    col_k[low, :] = col_of(s1_low * s1_low * s1_low * total * (1.0 / channels))
    over_tiles(lambda where, t: back_one_rows(where, t, low))
    short_back = halo(e0.at[:, pl.ds(0, 8), :], e0.at[:, pl.ds(256, 8), :], 1, preceding)

    for q in range(chunks):
        medium_back[q].wait_recv()

        @pl.when(k == kn - 1)
        def _(q=q):
            e1[ROWS : ROWS + HALF, part(q)] = jnp.zeros((HALF, WIDE), BF16)

        medium_adjoint(part(q), high)
    psh[3, me] = row_of(sums[high, :])
    sent_m1_high = exchange(psh.at[3], 6)
    over_tiles(lambda where, t: short_adjoint(where, t, 0, 112))
    local_part(a2, False)
    fore_three = scan_three(fore_two, r1_f, r2_f, o3_f, r3_f, 1, False)
    short_back.wait_recv()

    @pl.when(k == kn - 1)
    def _():
        e0[:, 256:264, :] = jnp.zeros((tiles, 8, LANE), F32)

    total = collect(sent_m1_high, psh.at[3])
    col_k[high, :] = col_of(s1_high * s1_high * s1_high * total * (1.0 / channels))
    over_tiles(lambda where, t: back_one_rows(where, t, high))
    over_tiles(lambda where, t: short_adjoint(where, t, 112, 144))
    ps0[1, me] = row_of(sums2[...])
    sent_m0 = exchange(ps0.at[1], 7)

    finish(fore_three)

    def fore_long(rows, where, value):
        conv = (local[rows, where] + value).astype(BF16).astype(F32)
        result = x2[rows, where].astype(F32) + post[2, rows, where].astype(F32) * conv
        out[rows, where] = result.astype(BF16)

    carried(r3_f, False, fore_long)
    store_out = pltpu.make_async_copy(out, both_h.at[0], store_sem.at[1])
    store_out.start()

    total = collect(sent_m0, ps0.at[1])
    col_k[...] = col_of(s0 * s0 * s0 * total * (1.0 / channels))

    def final_rows(where, t):
        value = (
            g1[:, where].astype(F32)
            + u0[:, where] * col_s[0]
            - x0[:, where].astype(F32) * col_k[...]
        )
        grad[:, where] = value.astype(BF16)

    over_tiles(final_rows)
    store_grad = pltpu.make_async_copy(grad, both_h.at[1], store_sem.at[0])
    store_grad.start()
    for copy in leaving:
        copy.wait_send()
    for copy, sends, gets in back_two + fore_two:

        @pl.when(sends)
        def _(copy=copy):
            copy.wait_send()

    store_out.wait()
    store_grad.wait()


def per_device(zn, tn, *args):
    stream, pre, post, gains, se, mr, res, dec, cot = args
    width = stream.shape[1]
    channels = width * tn
    tiles = width // LANE
    tables = (
        jnp.asarray(dft_matrix(WIDE, WIDE), BF16),
        jnp.asarray(dft_matrix(WIDE, WIDE).T * (2.0 / WIDE), BF16),
        jnp.asarray(dft_matrix(2 * ROWS, ROWS), BF16),
        jnp.asarray(dft_matrix(2 * ROWS, ROWS).T * (1.0 / ROWS), BF16),
    )
    operands = (stream, pre, post, gains, se, mr, res.T, dec.T, cot) + tables
    vmem = pltpu.VMEM
    whole = (ROWS, width)
    scan = (YN, POLES, WIDE)
    scratch = [vmem(o.shape, o.dtype) for o in operands]
    scratch += [
        vmem(whole, BF16),
        vmem(whole, BF16),
        vmem((tiles, ROWS + 8, LANE), F32),
        vmem((tiles, ROWS + 8, LANE), F32),
        vmem((ROWS + HALF, width), BF16),
        vmem((ROWS + HALF, width), BF16),
        vmem(whole, BF16),
        vmem(whole, BF16),
        vmem(whole, F32),
        vmem(whole, F32),
        vmem(whole, F32),
        vmem(whole, BF16),
        vmem(whole, BF16),
        vmem(whole, F32),
        vmem(whole, BF16),
        vmem(whole, BF16),
        vmem((POLES, width), F32),
        vmem((POLES, 8, width), F32),
        vmem((POLES, 8, width), F32),
        vmem(whole, F32),
        vmem((WIDE, width), F32),
        vmem((2 * ROWS, width), F32),
        vmem((HALF, width), BF16),
        vmem((HALF, width), BF16),
        vmem((2, 1, HALF), F32),
        vmem((HALF, LANE), F32),
        vmem((ROWS, LANE), F32),
        vmem((ROWS, LANE), F32),
        vmem((3, ROWS, LANE), F32),
        vmem((ROWS, LANE), F32),
        vmem((2, tn, 1, ROWS), F32),
        vmem((4, tn, 1, HALF), F32),
        vmem((tn, 2, ROWS), F32),
        vmem(scan, F32), vmem(scan, F32),
        vmem(scan, F32), vmem(scan, F32),
        vmem(scan[1:], F32), vmem(scan[1:], F32),
        vmem((zn, POLES, WIDE), F32), vmem((zn, POLES, WIDE), F32),
        vmem(scan, F32), vmem(scan, F32),
        vmem(scan, F32), vmem(scan, F32),
    ]
    sem = pltpu.SemaphoreType.DMA
    scratch += [
        sem((17,)), sem((2,)), sem((8, tn)), sem((8, tn)), sem((11,)), sem((11,)),
        sem((2, YN)), sem((2, YN)), sem((2, zn)), sem((2, zn)), sem((2, YN)), sem((2, YN)),
    ]
    any_spec = pl.BlockSpec(memory_space=pl.ANY)
    both = pl.pallas_call(
        functools.partial(kernel, zn, tn, channels),
        out_shape=jax.ShapeDtypeStruct((2,) + whole, BF16),
        in_specs=[any_spec] * len(operands),
        out_specs=any_spec,
        scratch_shapes=scratch,
        compiler_params=pltpu.CompilerParams(
            collective_id=0, has_side_effects=True, vmem_limit_bytes=60 * 2**20
        ),
        cost_estimate=pl.CostEstimate(
            flops=4_000_000_000, bytes_accessed=7_000_000, transcendentals=500_000
        ),
        name="hyena_group",
    )(*operands)
    return both[0], both[1]


def solution(mesh):
    zn = mesh.shape["context"] // YN
    tn = mesh.shape["tensor"]
    placed = (
        P("context", "tensor"),
        P(None, "context", "tensor"),
        P(None, "context", "tensor"),
        P(None, "tensor"),
        P(None, "tensor"),
        P(None, "tensor"),
        P("tensor", None),
        P("tensor", None),
        P("context", "tensor"),
    )
    return jax.shard_map(
        functools.partial(per_device, zn, tn),
        mesh=mesh,
        in_specs=placed,
        out_specs=(P("context", "tensor"), P("context", "tensor")),
        check_vma=False,
    )
```
